32 devices in a mesh: dp: 2 (over y), context: 16 (over z, x, core).
Axes of the slice: x: 2, y: 2, z: 4, core: 2. Of those that a mesh axis runs over, the one named last changes fastest.
Arguments:
- query_rows: bfloat16 [4096, 4096], P(('dp', 'context')), parts along dimension 0, may hold values from -6 to 6
- key_rows: bfloat16 [4096, 512], P(('dp', 'context')), parts along dimension 0, may hold values from -6 to 6
- value_rows: bfloat16 [4096, 512], P(('dp', 'context')), parts along dimension 0, may hold values from -6 to 6
- grad_out: bfloat16 [4096, 4096], P(('dp', 'context')), parts along dimension 0, may hold values from -6 to 6
- doc_bounds: int32 [10], P('dp'), parts along dimension 0, may hold values from 0 to 2048, as said below
Outputs:
- attn_out: bfloat16 [4096, 4096], P(('dp', 'context')), parts along dimension 0
- d_query: bfloat16 [4096, 4096], P(('dp', 'context')), parts along dimension 0
- d_key: bfloat16 [4096, 512], P(('dp', 'context')), parts along dimension 0
- d_value: bfloat16 [4096, 512], P(('dp', 'context')), parts along dimension 0
The draws below stay inside these ranges and needn't reach their ends.
There are 2 independent parts, one for each index of `dp`. The reference program is written for one: setup_inputs(seed, part) draws one part's arguments, and reference() takes and returns one part's arrays. A program takes and returns all parts, laid end to end along the dimension named above; each array names one. Nothing has to cross between parts.
Inputs may be any that keep to these rules, and one draw needn't show every extreme that they name: doc_bounds[0] = 0, doc_bounds[4] = 2048, strictly rising; every response is 256 to 1024 tokens long; at least one is exactly 1024 and at least one exactly 256.
All inputs are finite; a program needn't handle non-finite values.
Results may differ from the reference program's by a relative error of at most 0.035.
Values may be sent and summed in bfloat16 or wider, within the bound.
No kernel may reach another device: no remote copies, remote signals or barrier semaphores. Data moves between devices by JAX's collectives and lax.ppermute only.
A program may use at most 64 MiB of HBM per device.

```python
import jax
import jax.numpy as jnp
from jax import lax

H = 32
KVH = 4
HEAD_DIM = 128
MINDOC = 256
MAXDOC = 1024
QBLOCK = 512
TOKENS = 2048
NDOC = 4


def draw_query_rows(key, part):
    key = jax.random.fold_in(key, 11)
    rows = jnp.clip(1.5 * jax.random.normal(key, (TOKENS, H * HEAD_DIM), jnp.float32), -6.0, 6.0)
    return rows.astype(jnp.bfloat16)


def draw_key_rows(key, part):
    key = jax.random.fold_in(key, 23)
    rows = jnp.clip(jax.random.normal(key, (TOKENS, KVH * HEAD_DIM), jnp.float32), -6.0, 6.0)
    return rows.astype(jnp.bfloat16)


def draw_doc_bounds(key, part):
    key = jax.random.fold_in(key, 7)
    key_pair, key_special, key_order = jax.random.split(key, 3)
    half_count = NDOC // 2
    offsets = jax.random.randint(key_pair, (half_count,), 0, 2 * MINDOC + 1)
    first = MINDOC + offsets
    second = 3 * MINDOC - offsets
    extra = jax.random.randint(key_special, (1,), 0, MINDOC + 1)
    special = jnp.concatenate([jnp.array([4 * MINDOC, MINDOC], jnp.int32), MINDOC + extra, 2 * MINDOC - extra])
    lengths = jnp.concatenate([special, first[2:], second[2:]]).astype(jnp.int32)
    lengths = lengths[jax.random.permutation(key_order, NDOC)]
    return jnp.concatenate([jnp.zeros((1,), jnp.int32), jnp.cumsum(lengths).astype(jnp.int32)])


def shard_levels(key, extent, shards, smallest, top_value):
    loudness, own = 1.0, jax.random.fold_in(key, 6)
    for dim, shards_of in shards:
        draws = jnp.exp(jax.random.uniform(jax.random.fold_in(own, dim), (shards_of,), jnp.float32, smallest / len(shards), top_value / len(shards)))
        loudness = loudness * jnp.repeat(draws, extent[dim] // shards_of).reshape([-1 if axis == dim else 1 for axis in range(len(extent))])
    return loudness


def normal_values(own_key, dims, scale, reach, shards=(), kind=jnp.bfloat16):
    gain = shard_levels(own_key, dims, shards, -0.22, 0.18) if shards else 1.0
    values = jax.random.normal(own_key, dims, jnp.float32) * scale * gain
    return jnp.minimum(jnp.maximum(values, -reach), reach).astype(kind)


def setup_inputs(seed: int = 0, part: int = 0) -> dict:
    key_of = jax.random.split(jax.random.key(seed), 6)
    own_keys = jax.random.split(jax.random.fold_in(key_of[5], part), 6)
    return {
        "query_rows": draw_query_rows(jax.random.fold_in(jax.random.fold_in(key_of[5], part), 71), part),
        "key_rows": draw_key_rows(jax.random.fold_in(jax.random.fold_in(key_of[5], part), 71), part),
        "value_rows": normal_values(own_keys[2], (TOKENS, KVH * HEAD_DIM), 1.0, 6.0, ((0, 16),)),
        "grad_out": normal_values(own_keys[3], (TOKENS, H * HEAD_DIM), 1.0, 6.0, ((0, 16),)),
        "doc_bounds": draw_doc_bounds(jax.random.fold_in(jax.random.fold_in(key_of[5], part), 71), part),
    }


masked_score = -1e30


def segment_ids(positions, doc_bounds):
    inner_bounds = doc_bounds[1:-1]
    return jnp.sum((positions[:, None] >= inner_bounds[None, :]).astype(jnp.int32), axis=1)


def block_pass(q_block, k_window, v_window, o_grad, allowed, softmax_scale):
    scores = jnp.einsum('qhd,kd->hqk', q_block.astype(jnp.float32), k_window.astype(jnp.float32)) * softmax_scale
    scores = jnp.where(allowed[None], scores, masked_score)
    top_score = jnp.max(scores, axis=-1, keepdims=True)
    expd = jnp.where(allowed[None], jnp.exp(scores - top_score), 0.0)
    probs = expd / jnp.sum(expd, axis=-1, keepdims=True)
    weights = probs.astype(jnp.bfloat16)
    attended = jnp.einsum('hqk,kd->qhd', weights.astype(jnp.float32), v_window.astype(jnp.float32)).astype(jnp.bfloat16)
    inner_prod = jnp.sum(o_grad.astype(jnp.float32) * attended.astype(jnp.float32), axis=-1)
    prob_grad = jnp.einsum('qhd,kd->hqk', o_grad.astype(jnp.float32), v_window.astype(jnp.float32))
    score_grad = (probs * (prob_grad - jnp.transpose(inner_prod)[:, :, None])).astype(jnp.bfloat16)
    q_grad = (softmax_scale * jnp.einsum('hqk,kd->qhd', score_grad.astype(jnp.float32), k_window.astype(jnp.float32))).astype(jnp.bfloat16)
    k_grad = softmax_scale * jnp.einsum('hqk,qhd->kd', score_grad.astype(jnp.float32), q_block.astype(jnp.float32))
    v_grad = jnp.einsum('hqk,qhd->kd', weights.astype(jnp.float32), o_grad.astype(jnp.float32))
    return attended, q_grad, k_grad, v_grad


def head_pass(q_heads, k_head, v_head, g_heads, doc_bounds, softmax_scale):
    length = q_heads.shape[0]
    width = k_head.shape[1]
    span = QBLOCK + MAXDOC
    k_pad = jnp.concatenate([jnp.zeros((MAXDOC, width), k_head.dtype), k_head], axis=0)
    v_pad = jnp.concatenate([jnp.zeros((MAXDOC, width), v_head.dtype), v_head], axis=0)
    seg_all = segment_ids(jnp.arange(length + MAXDOC, dtype=jnp.int32) - MAXDOC, doc_bounds)

    def step(carry, start):
        k_acc, v_acc = carry
        q_block = lax.dynamic_slice_in_dim(q_heads, start, QBLOCK, 0)
        g_block = lax.dynamic_slice_in_dim(g_heads, start, QBLOCK, 0)
        k_window = lax.dynamic_slice_in_dim(k_pad, start, span, 0)
        v_window = lax.dynamic_slice_in_dim(v_pad, start, span, 0)
        q_pos = start + jnp.arange(QBLOCK, dtype=jnp.int32)
        k_pos = start - MAXDOC + jnp.arange(span, dtype=jnp.int32)
        q_seg = lax.dynamic_slice_in_dim(seg_all, start + MAXDOC, QBLOCK, 0)
        k_seg = lax.dynamic_slice_in_dim(seg_all, start, span, 0)
        allowed = (q_seg[:, None] == k_seg[None, :]) & (k_pos[None, :] <= q_pos[:, None]) & (k_pos[None, :] >= 0)
        attended, q_grad, k_grad, v_grad = block_pass(q_block, k_window, v_window, g_block, allowed, softmax_scale)
        k_acc = lax.dynamic_update_slice_in_dim(k_acc, lax.dynamic_slice_in_dim(k_acc, start, span, 0) + k_grad, start, 0)
        v_acc = lax.dynamic_update_slice_in_dim(v_acc, lax.dynamic_slice_in_dim(v_acc, start, span, 0) + v_grad, start, 0)
        return (k_acc, v_acc), (attended, q_grad)

    starts = jnp.arange(0, length, QBLOCK, dtype=jnp.int32)
    empty = jnp.zeros((length + MAXDOC, width), jnp.float32)
    (k_acc, v_acc), (attended, q_grad) = lax.scan(step, (empty, empty), starts)
    heads_here = q_heads.shape[1]
    return (attended.reshape(length, heads_here, width), q_grad.reshape(length, heads_here, width),
            k_acc[MAXDOC:], v_acc[MAXDOC:])


def reference(query_rows, key_rows, value_rows, grad_out, doc_bounds):
    length = query_rows.shape[0]
    group = H // KVH
    softmax_scale = HEAD_DIM ** -0.5
    q_heads = query_rows.reshape(length, H, HEAD_DIM).transpose(1, 0, 2)
    g_heads = grad_out.reshape(length, H, HEAD_DIM).transpose(1, 0, 2)
    k_heads = key_rows.reshape(length, KVH, HEAD_DIM).transpose(1, 0, 2)
    v_heads = value_rows.reshape(length, KVH, HEAD_DIM).transpose(1, 0, 2)

    def one_head(inputs):
        q_one, g_one, head = inputs
        k_one = lax.dynamic_index_in_dim(k_heads, head // group, 0, keepdims=False)
        v_one = lax.dynamic_index_in_dim(v_heads, head // group, 0, keepdims=False)
        attended, q_grad, k_grad, v_grad = head_pass(q_one[:, None, :], k_one, v_one, g_one[:, None, :], doc_bounds, softmax_scale)
        return attended[:, 0], q_grad[:, 0], k_grad, v_grad

    attended, q_grad, k_grad, v_grad = lax.map(one_head, (q_heads, g_heads, jnp.arange(H, dtype=jnp.int32)))
    attn_out = attended.transpose(1, 0, 2).reshape(length, H * HEAD_DIM)
    d_query = q_grad.transpose(1, 0, 2).reshape(length, H * HEAD_DIM)
    d_key = k_grad.reshape(KVH, group, length, HEAD_DIM).sum(axis=1).transpose(1, 0, 2).reshape(length, KVH * HEAD_DIM)
    d_value = v_grad.reshape(KVH, group, length, HEAD_DIM).sum(axis=1).transpose(1, 0, 2).reshape(length, KVH * HEAD_DIM)
    return attn_out, d_query, d_key.astype(jnp.bfloat16), d_value.astype(jnp.bfloat16)
```

```python
import functools
import math

import jax
import jax.numpy as jnp
from jax import lax
from jax.experimental import pallas as pl
from jax.experimental.pallas import tpu as pltpu
from jax.sharding import PartitionSpec as P

HEAD_DIM = 128
MASKED = -1e30
CHUNKS = 5
NT = (((1,), (1,)), ((), ()))
NN = (((1,), (0,)), ((), ()))
BF = jnp.bfloat16
F32 = jnp.float32
VMEM = pl.BlockSpec(memory_space=pltpu.VMEM)
ANYWHERE = pl.BlockSpec(memory_space=pl.ANY)


def dot(a, b, dims=NN):
    return lax.dot_general(a, b, dims, preferred_element_type=F32)


def in_hbm(x):
    return pltpu.with_memory_space_constraint(x, pltpu.HBM)


def position():
    me = lax.axis_index("context").astype(jnp.int32)
    return lax.rem(me, 2), lax.div(me, 2)


def run(moves, sems):
    copies = [pltpu.make_async_copy(a, b, sems.at[i]) for i, (a, b) in enumerate(moves)]
    for copy in copies:
        copy.start()
    return copies


def share_kernel(k, v, q, g, own, theirs, sent, sems):
    core, _ = position()
    moves = []
    for out, owner, left, right in ((theirs, 1 - core, k, v), (own, core, k, v), (sent, 1 - core, q, g)):
        width = out.shape[1] // 2
        cols = pl.ds(pl.multiple_of(owner * width, width), width)
        moves += [
            (left.at[:, cols], out.at[:, pl.ds(0, width)]),
            (right.at[:, cols], out.at[:, pl.ds(width, width)]),
        ]
    for copy in run(moves, sems):
        copy.wait()


def payload_kernel(heads, kv_own, kv_oth, sent_in, sent, *kv):
    core, _ = position()
    rows = kv_own.shape[0]
    width = HEAD_DIM
    for block, part in ((core, kv_own), (1 - core, kv_oth)):
        at = pl.ds(pl.multiple_of(block * rows, rows), rows)
        for s, out in enumerate(kv):
            out[at, :width] = part[:, s * width:(s + 1) * width]
            out[at, width:] = part[:, (heads + s) * width:(heads + s + 1) * width]


def stage_kernel(
    heads, bounds_in, q_all, g_all, other, q_st, g_st, q_t, g_t, k_seg, q_own, g_own, bounds, sems
):
    core, chip = position()
    rows = q_own.shape[0]
    width = HEAD_DIM
    units = q_t.shape[0] // heads
    pairs = units // 2
    two = 2 * rows
    share = q_own.shape[1]
    own = pl.ds(pl.multiple_of(core * share, share), share)
    copies = run([(bounds_in, bounds), (q_all.at[:, own], q_own), (g_all.at[:, own], g_own)], sems)
    copies[0].wait()

    def segment(pos):
        seg = jnp.zeros(pos.shape, jnp.int32)
        for b in range(1, bounds.shape[0] - 1):
            seg += (pos >= bounds[b]).astype(jnp.int32)
        return seg

    sub = lax.broadcasted_iota(jnp.int32, (rows, width), 0)
    seg_lane = lax.broadcasted_iota(jnp.int32, (rows, width), 1)
    for b in range(2 * CHUNKS):
        pos = (2 * (chip + 1 - CHUNKS) + b) * rows + sub
        seg = jnp.where(pos >= 0, segment(pos), width - 1)
        k_seg[b * rows:(b + 1) * rows] = (seg_lane == seg).astype(BF)
    for copy in copies[1:]:
        copy.wait()
    for s in range(heads):
        for p in range(pairs):
            for i in range(2):
                col = ((s * pairs + p) * 2 + i) * width
                cols = slice(col, col + width)
                for block, q, g in ((core, q_own, g_own), (1 - core, other, other.at[:, pl.ds(share, share)])):
                    at = pl.multiple_of((s * units + block * pairs + p) * two + i * rows, rows)
                    q_st[pl.ds(at, rows)] = q[:, cols]
                    g_st[pl.ds(at, rows)] = g[:, cols]
    lane = lax.broadcasted_iota(jnp.int32, (width, two), 1)
    lane = jnp.where(lane >= rows, lane - rows, lane)
    row = lax.broadcasted_iota(jnp.int32, (width, two), 0)
    for block in range(2):
        away = jnp.where(row == segment((2 * chip + block) * rows + lane), 0.0, MASKED).astype(BF)
        for s in range(heads):
            for p in range(pairs):
                u = s * units + block * pairs + p
                q_t[u, :width] = q_st[u * two:(u + 1) * two].T
                q_t[u, width:] = away
                g_t[u] = g_st[u * two:(u + 1) * two].T


def attention_kernel(
    slot, heads, q_st, g_st, q_t, g_t, k_seg, kv4, kv_edge, kv2, kv_middle, kv0, *refs
):
    o_all, dq_all, sent, d4, d_edge, d2, d_middle, d0 = refs[-22:-14]
    (k_aug, v_win, k_t, v_t, qs_st, gs_st, s_scr, p_scr, d_scr, dk_acc, dv_acc, o_scr, dq_scr,
     sems) = refs[-14:]
    width = HEAD_DIM
    scale = width ** -0.5
    core, chip = position()
    units = q_t.shape[0] // heads
    pairs = units // 2
    two = q_t.shape[2]
    rows = two // 2
    wide = 2 * pairs * width
    blocks = 2 * CHUNKS - 1
    span = blocks * rows
    base = slot * units
    even = lax.rem(chip, 2) == 0
    edge = pl.multiple_of(jnp.where(even, two, 3 * two), two)
    middle = pl.multiple_of(jnp.where(even, 3 * two, two), two)
    places = [pl.ds(at, two) for at in (0, edge, 2 * two, middle, 4 * two)]

    k_aug[:, width:] = k_seg[...]
    for at, kv in zip(places, (kv4, kv_edge, kv2, kv_middle, kv0)):
        k_aug[at, :width] = kv[:, :width]
        v_win[at] = kv[:, width:]
        k_t[:, at] = kv[:, :width].T
        v_t[:width, at] = kv[:, width:].T

    v_t[width:] = jnp.ones((v_t.shape[0] - width, v_t.shape[1]), BF)

    lane = lax.broadcasted_iota(jnp.int32, (rows, two), 1)
    causal = lax.broadcasted_iota(jnp.int32, (rows, two), 0) <= jnp.where(lane >= rows, lane - rows, lane)

    def window(u):
        first = (u // pairs) * rows
        return first, slice(first, first + span)

    def columns(u):
        return slice(u * two, (u + 1) * two)

    def fold(x, op):
        return op(x.reshape(x.shape[0] // 8, 8, x.shape[1]), axis=0)

    def scores(u, b, top):
        first, _ = window(u)
        s = dot(k_aug[first + b * rows:first + (b + 3) * rows], q_t[base + u])
        for i in range(3):
            part = s[i * rows:(i + 1) * rows]
            if b + i == blocks - 1:
                part = jnp.where(causal, part, MASKED)
            s_scr[u % 2, (b + i) * rows:(b + i + 1) * rows] = part
            top = jnp.maximum(top, fold(part, jnp.max))
        return top

    def weights(u, b, peak):
        first, _ = window(u)
        e = jnp.exp2((s_scr[u % 2, b * rows:(b + 1) * rows] - peak) * (scale * math.log2(math.e)))
        p_scr[first + b * rows:first + (b + 1) * rows, columns(u)] = e.astype(BF)

    def score_grads(u, b, inner):
        first, _ = window(u)
        keys = slice(first + b * rows, first + (b + 3) * rows)
        dp = dot(v_win[keys], g_t[base + u])
        d_scr[keys, columns(u)] = p_scr[keys, columns(u)] * (dp - inner).astype(BF)

    def store(x, out, u):
        block, p = u // pairs, u % pairs
        x = x.T
        for i in range(2):
            out[block * rows:(block + 1) * rows, (2 * p + i) * width:(2 * p + i + 1) * width] = (
                x[i * rows:(i + 1) * rows]
            )

    def query_grad(u, inv):
        _, keys = window(u)
        store((dot(k_t[:, keys], d_scr[keys, columns(u)]) * (inv * scale)).astype(BF), dq_scr, u)

    half = pairs * two
    part = (3 * pairs // 2) * two
    sums = ((p_scr, gs_st, dv_acc), (d_scr, qs_st, dk_acc))
    first_group = [(b * rows, *one) for b in range(0, blocks, 3) for one in sums]
    second_group = [(rows + b * rows, *one) for b in range(0, blocks, 3) for one in sums]
    for _, _, acc in sums:
        acc[span:] = jnp.zeros((rows, width), F32)

    def key_grads(u):
        if u > pairs and first_group:
            at, left, right, acc = first_group.pop(0)
            at = slice(at, at + 3 * rows)
            acc[at] = dot(left[at, :half], right[:half])
        elif u > 3 * pairs // 2 and second_group:
            at, left, right, acc = second_group.pop(0)
            at = slice(at, at + 3 * rows)
            acc[at] += dot(left[at, half:part], right[half:part])

    def one_unit(u, peak, inv_before, more):
        _, keys = window(u)
        top = jnp.full((8, two), MASKED, F32)
        for b in range(0, blocks, 3):
            if more:
                top = scores(u + 1, b, top)
            key_grads(u)
            for i in range(3):
                weights(u, b + i, peak)
        peak = jnp.max(top, axis=0, keepdims=True)
        o = dot(v_t[:, keys], p_scr[keys, columns(u)])
        if u > 0:
            query_grad(u - 1, inv_before)
        inv = 1.0 / o[width:width + 1]
        o = (o[:width] * inv).astype(BF)
        store(o, o_scr, u)
        inner = jnp.sum(g_t[base + u].astype(F32) * o.astype(F32), axis=0, keepdims=True)
        for b in range(0, blocks, 3):
            key_grads(u)
            score_grads(u, b, inner)
        column = jnp.broadcast_to(inv, (8, two)).T[:, :1]
        here, there = slice(u * two, (u + 1) * two), slice((base + u) * two, (base + u + 1) * two)
        qs_st[here] = (q_st[there].astype(F32) * column).astype(BF)
        gs_st[here] = (g_st[there].astype(F32) * column).astype(BF)
        return peak, inv

    top = jnp.full((8, two), MASKED, F32)
    for b in range(0, blocks, 3):
        top = scores(0, b, top)
    peak, inv = jnp.max(top, axis=0, keepdims=True), None
    for u in range(units):
        peak, inv = one_unit(u, peak, inv, u + 1 < units)
    query_grad(units - 1, inv)

    mine = pl.ds(pl.multiple_of(core * rows, rows), rows)
    other = pl.ds(pl.multiple_of((1 - core) * rows, rows), rows)
    cols = pl.ds(pl.multiple_of((core * heads + slot) * wide, wide), wide)
    moves = [
        (o_scr.at[other], sent.at[:, pl.ds(0, wide)]),
        (dq_scr.at[other], sent.at[:, pl.ds(wide, wide)]),
        (o_scr.at[mine], o_all.at[:, cols]),
        (dq_scr.at[mine], dq_all.at[:, cols]),
    ]
    copies = run(moves, sems)

    for left, right, acc, factor, col in (
        (d_scr, qs_st, dk_acc, scale, 0), (p_scr, gs_st, dv_acc, 1.0, width)
    ):
        cols = slice(col, col + width)

        def total(keys):
            return factor * (acc[keys] + dot(left[keys, part:], right[part:]))

        d4[:rows, cols] = (factor * acc[:rows]).astype(d4.dtype)
        d4[rows:, cols] = total(slice(rows, two)).astype(d4.dtype)
        for at, out in zip(places[1:], (d_edge, d2, d_middle, d0)):
            out[:, cols] = total(at).astype(out.dtype)
    for copy in copies:
        copy.wait()


def place_kernel(heads, o_in, dq_in, *refs):
    backs = refs[:heads]
    mine, theirs, o, dq, dk, dv, sems = refs[heads:]
    core, _ = position()
    wide = backs[0].shape[1] // 2
    half = mine.shape[1] // 2
    moves = []
    for s, back in enumerate(backs):
        cols = pl.ds(pl.multiple_of(((1 - core) * heads + s) * wide, wide), wide)
        moves += [(back.at[:, pl.ds(0, wide)], o.at[:, cols]), (back.at[:, pl.ds(wide, wide)], dq.at[:, cols])]
    for part, owner in ((mine, core), (theirs, 1 - core)):
        cols = pl.ds(pl.multiple_of(owner * half, half), half)
        moves += [(part.at[:, pl.ds(0, half)], dk.at[:, cols]), (part.at[:, pl.ds(half, half)], dv.at[:, cols])]
    for copy in run(moves, sems):
        copy.wait()


def shares(k, v, q, g):
    return pl.pallas_call(
        share_kernel,
        in_specs=[ANYWHERE] * 4,
        out_specs=[VMEM] * 3,
        out_shape=[jax.ShapeDtypeStruct(x.shape, BF) for x in (k, v, q)],
        scratch_shapes=[pltpu.SemaphoreType.DMA((6,))],
        compiler_params=pltpu.CompilerParams(vmem_limit_bytes=4 * 1024 * 1024),
        name="share",
    )(in_hbm(k), in_hbm(v), in_hbm(q), in_hbm(g))


def payloads(kv_own, kv_oth, sent, heads):
    kv = jax.ShapeDtypeStruct((2 * kv_own.shape[0], 2 * HEAD_DIM), BF)
    return pl.pallas_call(
        functools.partial(payload_kernel, heads),
        in_specs=[VMEM] * 2 + [ANYWHERE],
        out_specs=[ANYWHERE] + [VMEM] * heads,
        out_shape=[jax.ShapeDtypeStruct(sent.shape, BF)] + [kv] * heads,
        input_output_aliases={2: 0},
        compiler_params=pltpu.CompilerParams(vmem_limit_bytes=4 * 1024 * 1024),
        name="payload",
    )(kv_own, kv_oth, sent)


def staged(bounds, q, g, other, heads):
    rows = q.shape[0]
    width = HEAD_DIM
    units = q.shape[1] // (2 * width)
    return pl.pallas_call(
        functools.partial(stage_kernel, heads),
        in_specs=[ANYWHERE, ANYWHERE, ANYWHERE, VMEM],
        out_specs=[VMEM] * 5,
        out_shape=[
            jax.ShapeDtypeStruct((units * 2 * rows, width), BF),
            jax.ShapeDtypeStruct((units * 2 * rows, width), BF),
            jax.ShapeDtypeStruct((units, 2 * width, 2 * rows), BF),
            jax.ShapeDtypeStruct((units, width, 2 * rows), BF),
            jax.ShapeDtypeStruct((2 * CHUNKS * rows, width), BF),
        ],
        scratch_shapes=[
            pltpu.VMEM((rows, q.shape[1] // 2), BF),
            pltpu.VMEM((rows, q.shape[1] // 2), BF),
            pltpu.SMEM(bounds.shape, jnp.int32),
            pltpu.SemaphoreType.DMA((3,)),
        ],
        compiler_params=pltpu.CompilerParams(vmem_limit_bytes=16 * 1024 * 1024),
        cost_estimate=pl.CostEstimate(flops=0, bytes_accessed=8 * q.size, transcendentals=0),
        name="stage",
    )(in_hbm(bounds), in_hbm(q), in_hbm(g), other)


def head_attention(slot, heads, q, stage, window, so_far):
    rows = q.shape[0]
    width = HEAD_DIM
    two = 2 * rows
    units = stage[2].shape[0] // heads
    wide = q.shape[1] // (2 * heads)
    span = CHUNKS * two
    short = span - rows
    chunk = window[0].shape
    return pl.pallas_call(
        functools.partial(attention_kernel, slot, heads),
        in_specs=[VMEM] * 10 + [ANYWHERE] * len(so_far),
        out_specs=[ANYWHERE] * 3 + [VMEM] * 5,
        scratch_shapes=[
            pltpu.VMEM((span, 2 * width), BF),
            pltpu.VMEM((span, width), BF),
            pltpu.VMEM((width, span), BF),
            pltpu.VMEM((width + 16, span), BF),
            pltpu.VMEM((units * two, width), BF),
            pltpu.VMEM((units * two, width), BF),
            pltpu.VMEM((2, short, two), F32),
            pltpu.VMEM((span, units * two), BF),
            pltpu.VMEM((span, units * two), BF),
            pltpu.VMEM((span, width), F32),
            pltpu.VMEM((span, width), F32),
            pltpu.VMEM((two, wide), BF),
            pltpu.VMEM((two, wide), BF),
            pltpu.SemaphoreType.DMA((4,)),
        ],
        out_shape=[
            jax.ShapeDtypeStruct(q.shape, BF),
            jax.ShapeDtypeStruct(q.shape, BF),
            jax.ShapeDtypeStruct((rows, 2 * wide), BF),
        ] + [jax.ShapeDtypeStruct(chunk, t) for t in (BF, BF, F32, BF, F32)],
        input_output_aliases={10 + i: i for i in range(len(so_far))},
        compiler_params=pltpu.CompilerParams(vmem_limit_bytes=36 * 1024 * 1024),
        cost_estimate=pl.CostEstimate(
            flops=20 * rows * span * wide,
            bytes_accessed=24 * rows * wide,
            transcendentals=2 * rows * span * wide // width,
        ),
        name="attention%d" % slot,
    )(*stage, *window, *so_far)


def place(o, dq, backs, mine, theirs):
    heads = len(backs)
    return pl.pallas_call(
        functools.partial(place_kernel, heads),
        in_specs=[ANYWHERE] * (4 + heads),
        out_specs=[ANYWHERE] * 4,
        scratch_shapes=[pltpu.SemaphoreType.DMA((2 * heads + 4,))],
        out_shape=[
            jax.ShapeDtypeStruct(o.shape, BF),
            jax.ShapeDtypeStruct(dq.shape, BF),
            jax.ShapeDtypeStruct(mine.shape, BF),
            jax.ShapeDtypeStruct(mine.shape, BF),
        ],
        input_output_aliases={0: 0, 1: 1},
        compiler_params=pltpu.CompilerParams(vmem_limit_bytes=1024 * 1024),
        name="place",
    )(o, dq, *backs, mine, theirs)


def body(query_rows, key_rows, value_rows, grad_out, doc_bounds):
    core, chip = position()
    n = lax.axis_size("context")
    even = lax.rem(chip, 2) == 0
    rows = query_rows.shape[0]
    width = HEAD_DIM
    heads = key_rows.shape[1] // (2 * width)

    def shift(x, by):
        return lax.ppermute(x, "context", [(i, (i + by) % n) for i in range(n)])

    def swap(x):
        return lax.ppermute(x, "context", [(i, i ^ 1) for i in range(n)])

    def across(x):
        return lax.ppermute(x, "context", [(i, i ^ 2) for i in range(n)])

    kv_own, kv_sent, sent = shares(key_rows, value_rows, query_rows, grad_out)
    sent, *kv = payloads(kv_own, swap(kv_sent), sent, heads)
    stage = staged(doc_bounds, query_rows, grad_out, swap(sent), heads)

    o, dq, outs = None, None, []
    for s in range(heads):
        back2 = shift(kv[s], 4)
        edge = shift(jnp.where(even, kv[s], back2), 2)
        middle = across(back2)
        back4 = shift(back2, 4)
        o, dq, *rest = head_attention(
            s, heads, query_rows, stage, (back4, edge, back2, middle, kv[s]), () if s == 0 else (o, dq)
        )
        outs.append(rest)
    grads, backs = [], []
    for sent, d4, d_edge, d2, d_middle, d0 in outs:
        from_edge = shift(d_edge, -2)
        from_four = shift(d4, -4)
        from_middle = across(d_middle)
        d2 = jnp.where(even, d2, d2 + from_edge)
        from_two = shift((d2 + from_middle + from_four).astype(BF), -4)
        total = jnp.where(even, d0 + from_edge, d0) + from_two.astype(F32)
        grads.append(total.astype(BF))
        backs.append(swap(sent))
    total = jnp.concatenate([g[:, :width] for g in grads] + [g[:, width:] for g in grads], axis=1)
    mine = lax.dynamic_slice_in_dim(total, core * rows, rows, 0)
    theirs = swap(lax.dynamic_slice_in_dim(total, (1 - core) * rows, rows, 0))
    return place(o, dq, backs, mine, theirs)


def solution(mesh):
    rows = P(("dp", "context"), None)
    return jax.shard_map(
        body,
        mesh=mesh,
        in_specs=(rows, rows, rows, rows, P("dp")),
        out_specs=(rows, rows, rows, rows),
        check_vma=False,
    )
```

```python
import functools
import math

import jax
import jax.numpy as jnp
from jax import lax
from jax.experimental import pallas as pl
from jax.experimental.pallas import tpu as pltpu
from jax.sharding import PartitionSpec as P

HEAD_DIM = 128
MASKED = -1e30
CHUNKS = 5
NT = (((1,), (1,)), ((), ()))
NN = (((1,), (0,)), ((), ()))
BF = jnp.bfloat16
F32 = jnp.float32
VMEM = pl.BlockSpec(memory_space=pltpu.VMEM)
ANYWHERE = pl.BlockSpec(memory_space=pl.ANY)


def dot(a, b, dims=NN):
    return lax.dot_general(a, b, dims, preferred_element_type=F32)


def in_hbm(x):
    return pltpu.with_memory_space_constraint(x, pltpu.HBM)


def position():
    me = lax.axis_index("context").astype(jnp.int32)
    return lax.rem(me, 2), lax.div(me, 2)


def run(moves, sems):
    copies = [pltpu.make_async_copy(a, b, sems.at[i]) for i, (a, b) in enumerate(moves)]
    for copy in copies:
        copy.start()
    return copies


def share_kernel(k, v, q, g, own, theirs, sent, sems):
    core, _ = position()
    moves = []
    for out, owner, left, right in ((theirs, 1 - core, k, v), (own, core, k, v), (sent, 1 - core, q, g)):
        width = out.shape[1] // 2
        cols = pl.ds(pl.multiple_of(owner * width, width), width)
        moves += [
            (left.at[:, cols], out.at[:, pl.ds(0, width)]),
            (right.at[:, cols], out.at[:, pl.ds(width, width)]),
        ]
    for copy in run(moves, sems):
        copy.wait()


def payload_kernel(heads, kv_own, kv_oth, sent_in, sent, *kv):
    core, _ = position()
    rows = kv_own.shape[0]
    width = HEAD_DIM
    for block, part in ((core, kv_own), (1 - core, kv_oth)):
        at = pl.ds(pl.multiple_of(block * rows, rows), rows)
        for s, out in enumerate(kv):
            out[at, :width] = part[:, s * width:(s + 1) * width]
            out[at, width:] = part[:, (heads + s) * width:(heads + s + 1) * width]


def stage_kernel(
    heads, bounds_in, q_all, g_all, other, q_st, g_st, q_t, g_t, k_seg, q_own, g_own, bounds, sems
):
    core, chip = position()
    rows = q_own.shape[0]
    width = HEAD_DIM
    units = q_t.shape[0] // heads
    pairs = units // 2
    two = 2 * rows
    share = q_own.shape[1]
    own = pl.ds(pl.multiple_of(core * share, share), share)
    copies = run([(bounds_in, bounds), (q_all.at[:, own], q_own), (g_all.at[:, own], g_own)], sems)
    copies[0].wait()

    def segment(pos):
        seg = jnp.zeros(pos.shape, jnp.int32)
        for b in range(1, bounds.shape[0] - 1):
            seg += (pos >= bounds[b]).astype(jnp.int32)
        return seg

    sub = lax.broadcasted_iota(jnp.int32, (rows, width), 0)
    seg_lane = lax.broadcasted_iota(jnp.int32, (rows, width), 1)
    for b in range(2 * CHUNKS):
        pos = (2 * (chip + 1 - CHUNKS) + b) * rows + sub
        seg = jnp.where(pos >= 0, segment(pos), width - 1)
        k_seg[b * rows:(b + 1) * rows] = (seg_lane == seg).astype(BF)
    for copy in copies[1:]:
        copy.wait()
    for s in range(heads):
        for p in range(pairs):
            for i in range(2):
                col = ((s * pairs + p) * 2 + i) * width
                cols = slice(col, col + width)
                for block, q, g in ((core, q_own, g_own), (1 - core, other, other.at[:, pl.ds(share, share)])):
                    at = pl.multiple_of((s * units + block * pairs + p) * two + i * rows, rows)
                    q_st[pl.ds(at, rows)] = q[:, cols]
                    g_st[pl.ds(at, rows)] = g[:, cols]
    lane = lax.broadcasted_iota(jnp.int32, (width, two), 1)
    lane = jnp.where(lane >= rows, lane - rows, lane)
    row = lax.broadcasted_iota(jnp.int32, (width, two), 0)
    for block in range(2):
        away = jnp.where(row == segment((2 * chip + block) * rows + lane), 0.0, MASKED).astype(BF)
        for s in range(heads):
            for p in range(pairs):
                u = s * units + block * pairs + p
                q_t[u, :width] = q_st[u * two:(u + 1) * two].T
                q_t[u, width:] = away
                g_t[u] = g_st[u * two:(u + 1) * two].T


def attention_kernel(
    slot, heads, q_st, g_st, q_t, g_t, k_seg, kv4, kv_edge, kv2, kv_middle, kv0, *refs
):
    o_all, dq_all, sent, d4, d_edge, d2, d_middle, d0 = refs[-22:-14]
    (k_aug, v_win, k_t, v_t, qs_st, gs_st, s_scr, p_scr, d_scr, dk_acc, dv_acc, o_scr, dq_scr,
     sems) = refs[-14:]
    width = HEAD_DIM
    scale = width ** -0.5
    core, chip = position()
    units = q_t.shape[0] // heads
    pairs = units // 2
    two = q_t.shape[2]
    rows = two // 2
    wide = 2 * pairs * width
    base = slot * units
    half = pairs * two
    part = (3 * pairs // 2) * two
    sums = ((d_scr, qs_st, dk_acc, scale, 0), (p_scr, gs_st, dv_acc, 1.0, width))
    even = lax.rem(chip, 2) == 0
    edge = pl.multiple_of(jnp.where(even, two, 3 * two), two)
    middle = pl.multiple_of(jnp.where(even, 3 * two, two), two)
    places = [pl.ds(at, two) for at in (0, edge, 2 * two, middle, 4 * two)]

    def attend(blocks, step):
        whole = blocks == 2 * CHUNKS - 1
        k_aug[:, width:] = k_seg[...]
        for at, kv in zip(places, (kv4, kv_edge, kv2, kv_middle, kv0)):
            k_aug[at, :width] = kv[:, :width]
            v_win[at] = kv[:, width:]
            k_t[:, at] = kv[:, :width].T
            v_t[:width, at] = kv[:, width:].T

        v_t[width:] = jnp.ones((v_t.shape[0] - width, v_t.shape[1]), BF)

        lane = lax.broadcasted_iota(jnp.int32, (rows, two), 1)
        causal = lax.broadcasted_iota(jnp.int32, (rows, two), 0) <= jnp.where(lane >= rows, lane - rows, lane)

        def window(u):
            first = (u // pairs + 2 * CHUNKS - 1 - blocks) * rows
            return first, slice(first, first + blocks * rows)

        def columns(u):
            return slice(u * two, (u + 1) * two)

        def fold(x, op):
            return op(x.reshape(x.shape[0] // 8, 8, x.shape[1]), axis=0)

        def scores(u, b, top):
            first, _ = window(u)
            s = dot(k_aug[first + b * rows:first + (b + step) * rows], q_t[base + u])
            for i in range(step):
                part = s[i * rows:(i + 1) * rows]
                if b + i == blocks - 1:
                    part = jnp.where(causal, part, MASKED)
                s_scr[u % 2, (b + i) * rows:(b + i + 1) * rows] = part
                top = jnp.maximum(top, fold(part, jnp.max))
            return top

        def weights(u, b, peak):
            first, _ = window(u)
            e = jnp.exp2((s_scr[u % 2, b * rows:(b + 1) * rows] - peak) * (scale * math.log2(math.e)))
            p_scr[first + b * rows:first + (b + 1) * rows, columns(u)] = e.astype(BF)

        def score_grads(u, b, inner):
            first, _ = window(u)
            keys = slice(first + b * rows, first + (b + step) * rows)
            dp = dot(v_win[keys], g_t[base + u])
            d_scr[keys, columns(u)] = p_scr[keys, columns(u)] * (dp - inner).astype(BF)

        def store(x, out, u):
            block, p = u // pairs, u % pairs
            x = x.T
            for i in range(2):
                out[block * rows:(block + 1) * rows, (2 * p + i) * width:(2 * p + i + 1) * width] = (
                    x[i * rows:(i + 1) * rows]
                )

        def query_grad(u, inv):
            _, keys = window(u)
            store((dot(k_t[:, keys], d_scr[keys, columns(u)]) * (inv * scale)).astype(BF), dq_scr, u)

        first_group = [(b * rows, *one[:3]) for b in range(0, blocks, 3) for one in sums] if whole else []
        second_group = [(rows + b * rows, *one[:3]) for b in range(0, blocks, 3) for one in sums] if whole else []

        def key_grads(turn):
            if turn > pairs and first_group:
                at, left, right, acc = first_group.pop(0)
                at = slice(at, at + 3 * rows)
                acc[at] = dot(left[at, :half], right[:half])
            elif turn > 3 * pairs // 2 and second_group:
                at, left, right, acc = second_group.pop(0)
                at = slice(at, at + 3 * rows)
                acc[at] += dot(left[at, half:part], right[half:part])

        def outputs(u):
            _, keys = window(u)
            o = dot(v_t[:, keys], p_scr[keys, columns(u)])
            inv = 1.0 / o[width:width + 1]
            o = (o[:width] * inv).astype(BF)
            store(o, o_scr, u)
            inner = jnp.sum(g_t[base + u].astype(F32) * o.astype(F32), axis=0, keepdims=True)
            column = jnp.broadcast_to(inv, (8, two)).T[:, :1]
            here, there = slice(u * two, (u + 1) * two), slice((base + u) * two, (base + u + 1) * two)
            qs_st[here] = (q_st[there].astype(F32) * column).astype(BF)
            gs_st[here] = (g_st[there].astype(F32) * column).astype(BF)
            return inv, inner

        def turn(u, peak, inv, inner):
            top = jnp.full((8, two), MASKED, F32)
            for b in range(0, blocks, step):
                if u + 1 < units:
                    top = scores(u + 1, b, top)
                if 0 <= u < units:
                    for i in range(step):
                        weights(u, b + i, peak)
                if u > 0:
                    score_grads(u - 1, b, inner)
                key_grads(u)
                if u + 1 >= units:
                    key_grads(u)
            if u > 0:
                query_grad(u - 1, inv)
            if 0 <= u < units:
                inv, inner = outputs(u)
            return jnp.max(top, axis=0, keepdims=True), inv, inner

        if whole:
            for one in sums:
                one[2][blocks * rows:] = jnp.zeros((rows, width), F32)
        state = (None, None, None)
        for u in range(-1, units + 1):
            state = turn(u, *state)

        mine = pl.ds(pl.multiple_of(core * rows, rows), rows)
        other = pl.ds(pl.multiple_of((1 - core) * rows, rows), rows)
        cols = pl.ds(pl.multiple_of((core * heads + slot) * wide, wide), wide)
        moves = [
            (o_scr.at[other], sent.at[:, pl.ds(0, wide)]),
            (dq_scr.at[other], sent.at[:, pl.ds(wide, wide)]),
            (o_scr.at[mine], o_all.at[:, cols]),
            (dq_scr.at[mine], dq_all.at[:, cols]),
        ]
        copies = run(moves, sems)

        for left, right, acc, factor, col in sums:
            cols = slice(col, col + width)
            late = 3 * two
            if not whole:
                acc[:late] = jnp.zeros((late, width), F32)
                acc[late:] = dot(left[late:, half:], right[half:])
                acc[late:late + 3 * rows] += dot(left[late:late + 3 * rows, :half], right[:half])

            def total(keys):
                return factor * (acc[keys] + dot(left[keys, part:], right[part:]) if whole else acc[keys])

            d4[:rows, cols] = (factor * acc[:rows]).astype(d4.dtype)
            d4[rows:, cols] = total(slice(rows, two)).astype(d4.dtype)
            for at, out in zip(places[1:], (d_edge, d2, d_middle, d0)):
                out[:, cols] = total(at).astype(out.dtype)
        for copy in copies:
            copy.wait()

    @pl.when(chip >= 2)
    def _():
        attend(2 * CHUNKS - 1, 3)

    @pl.when(chip < 2)
    def _():
        attend(4, 2)


def place_kernel(heads, o_in, dq_in, *refs):
    backs = refs[:heads]
    mine, theirs, o, dq, dk, dv, sems = refs[heads:]
    core, _ = position()
    wide = backs[0].shape[1] // 2
    half = mine.shape[1] // 2
    moves = []
    for s, back in enumerate(backs):
        cols = pl.ds(pl.multiple_of(((1 - core) * heads + s) * wide, wide), wide)
        moves += [(back.at[:, pl.ds(0, wide)], o.at[:, cols]), (back.at[:, pl.ds(wide, wide)], dq.at[:, cols])]
    for part, owner in ((mine, core), (theirs, 1 - core)):
        cols = pl.ds(pl.multiple_of(owner * half, half), half)
        moves += [(part.at[:, pl.ds(0, half)], dk.at[:, cols]), (part.at[:, pl.ds(half, half)], dv.at[:, cols])]
    for copy in run(moves, sems):
        copy.wait()


def shares(k, v, q, g):
    return pl.pallas_call(
        share_kernel,
        in_specs=[ANYWHERE] * 4,
        out_specs=[VMEM] * 3,
        out_shape=[jax.ShapeDtypeStruct(x.shape, BF) for x in (k, v, q)],
        scratch_shapes=[pltpu.SemaphoreType.DMA((6,))],
        compiler_params=pltpu.CompilerParams(vmem_limit_bytes=4 * 1024 * 1024),
        name="share",
    )(in_hbm(k), in_hbm(v), in_hbm(q), in_hbm(g))


def payloads(kv_own, kv_oth, sent, heads):
    kv = jax.ShapeDtypeStruct((2 * kv_own.shape[0], 2 * HEAD_DIM), BF)
    return pl.pallas_call(
        functools.partial(payload_kernel, heads),
        in_specs=[VMEM] * 2 + [ANYWHERE],
        out_specs=[ANYWHERE] + [VMEM] * heads,
        out_shape=[jax.ShapeDtypeStruct(sent.shape, BF)] + [kv] * heads,
        input_output_aliases={2: 0},
        compiler_params=pltpu.CompilerParams(vmem_limit_bytes=4 * 1024 * 1024),
        name="payload",
    )(kv_own, kv_oth, sent)


def staged(bounds, q, g, other, heads):
    rows = q.shape[0]
    width = HEAD_DIM
    units = q.shape[1] // (2 * width)
    return pl.pallas_call(
        functools.partial(stage_kernel, heads),
        in_specs=[ANYWHERE, ANYWHERE, ANYWHERE, VMEM],
        out_specs=[VMEM] * 5,
        out_shape=[
            jax.ShapeDtypeStruct((units * 2 * rows, width), BF),
            jax.ShapeDtypeStruct((units * 2 * rows, width), BF),
            jax.ShapeDtypeStruct((units, 2 * width, 2 * rows), BF),
            jax.ShapeDtypeStruct((units, width, 2 * rows), BF),
            jax.ShapeDtypeStruct((2 * CHUNKS * rows, width), BF),
        ],
        scratch_shapes=[
            pltpu.VMEM((rows, q.shape[1] // 2), BF),
            pltpu.VMEM((rows, q.shape[1] // 2), BF),
            pltpu.SMEM(bounds.shape, jnp.int32),
            pltpu.SemaphoreType.DMA((3,)),
        ],
        compiler_params=pltpu.CompilerParams(vmem_limit_bytes=16 * 1024 * 1024),
        cost_estimate=pl.CostEstimate(flops=0, bytes_accessed=8 * q.size, transcendentals=0),
        name="stage",
    )(in_hbm(bounds), in_hbm(q), in_hbm(g), other)


def head_attention(slot, heads, q, stage, window, so_far):
    rows = q.shape[0]
    width = HEAD_DIM
    two = 2 * rows
    units = stage[2].shape[0] // heads
    wide = q.shape[1] // (2 * heads)
    span = CHUNKS * two
    short = span - rows
    chunk = window[0].shape
    return pl.pallas_call(
        functools.partial(attention_kernel, slot, heads),
        in_specs=[VMEM] * 10 + [ANYWHERE] * len(so_far),
        out_specs=[ANYWHERE] * 3 + [VMEM] * 5,
        scratch_shapes=[
            pltpu.VMEM((span, 2 * width), BF),
            pltpu.VMEM((span, width), BF),
            pltpu.VMEM((width, span), BF),
            pltpu.VMEM((width + 16, span), BF),
            pltpu.VMEM((units * two, width), BF),
            pltpu.VMEM((units * two, width), BF),
            pltpu.VMEM((2, short, two), F32),
            pltpu.VMEM((span, units * two), BF),
            pltpu.VMEM((span, units * two), BF),
            pltpu.VMEM((span, width), F32),
            pltpu.VMEM((span, width), F32),
            pltpu.VMEM((two, wide), BF),
            pltpu.VMEM((two, wide), BF),
            pltpu.SemaphoreType.DMA((4,)),
        ],
        out_shape=[
            jax.ShapeDtypeStruct(q.shape, BF),
            jax.ShapeDtypeStruct(q.shape, BF),
            jax.ShapeDtypeStruct((rows, 2 * wide), BF),
        ] + [jax.ShapeDtypeStruct(chunk, t) for t in (BF, BF, F32, BF, F32)],
        input_output_aliases={10 + i: i for i in range(len(so_far))},
        compiler_params=pltpu.CompilerParams(vmem_limit_bytes=36 * 1024 * 1024),
        cost_estimate=pl.CostEstimate(
            flops=20 * rows * span * wide,
            bytes_accessed=24 * rows * wide,
            transcendentals=2 * rows * span * wide // width,
        ),
        name="attention%d" % slot,
    )(*stage, *window, *so_far)


def place(o, dq, backs, mine, theirs):
    heads = len(backs)
    return pl.pallas_call(
        functools.partial(place_kernel, heads),
        in_specs=[ANYWHERE] * (4 + heads),
        out_specs=[ANYWHERE] * 4,
        scratch_shapes=[pltpu.SemaphoreType.DMA((2 * heads + 4,))],
        out_shape=[
            jax.ShapeDtypeStruct(o.shape, BF),
            jax.ShapeDtypeStruct(dq.shape, BF),
            jax.ShapeDtypeStruct(mine.shape, BF),
            jax.ShapeDtypeStruct(mine.shape, BF),
        ],
        input_output_aliases={0: 0, 1: 1},
        compiler_params=pltpu.CompilerParams(vmem_limit_bytes=1024 * 1024),
        name="place",
    )(o, dq, *backs, mine, theirs)


def body(query_rows, key_rows, value_rows, grad_out, doc_bounds):
    core, chip = position()
    n = lax.axis_size("context")
    even = lax.rem(chip, 2) == 0
    rows = query_rows.shape[0]
    width = HEAD_DIM
    heads = key_rows.shape[1] // (2 * width)

    def shift(x, by):
        return lax.ppermute(x, "context", [(i, (i + by) % n) for i in range(n)])

    def swap(x):
        return lax.ppermute(x, "context", [(i, i ^ 1) for i in range(n)])

    def across(x):
        return lax.ppermute(x, "context", [(i, i ^ 2) for i in range(n)])

    kv_own, kv_sent, sent = shares(key_rows, value_rows, query_rows, grad_out)
    sent, *kv = payloads(kv_own, swap(kv_sent), sent, heads)
    stage = staged(doc_bounds, query_rows, grad_out, swap(sent), heads)

    o, dq, outs = None, None, []
    for s in range(heads):
        back2 = shift(kv[s], 4)
        edge = shift(jnp.where(even, kv[s], back2), 2)
        middle = across(back2)
        back4 = shift(back2, 4)
        o, dq, *rest = head_attention(
            s, heads, query_rows, stage, (back4, edge, back2, middle, kv[s]), () if s == 0 else (o, dq)
        )
        outs.append(rest)
    grads, backs = [], []
    for sent, d4, d_edge, d2, d_middle, d0 in outs:
        from_edge = shift(d_edge, -2)
        from_four = shift(d4, -4)
        from_middle = across(d_middle)
        d2 = jnp.where(even, d2, d2 + from_edge)
        from_two = shift((d2 + from_middle + from_four).astype(BF), -4)
        total = jnp.where(even, d0 + from_edge, d0) + from_two.astype(F32)
        grads.append(total.astype(BF))
        backs.append(swap(sent))
    total = jnp.concatenate([g[:, :width] for g in grads] + [g[:, width:] for g in grads], axis=1)
    mine = lax.dynamic_slice_in_dim(total, core * rows, rows, 0)
    theirs = swap(lax.dynamic_slice_in_dim(total, (1 - core) * rows, rows, 0))
    return place(o, dq, backs, mine, theirs)


def solution(mesh):
    rows = P(("dp", "context"), None)
    return jax.shard_map(
        body,
        mesh=mesh,
        in_specs=(rows, rows, rows, rows, P("dp")),
        out_specs=(rows, rows, rows, rows),
        check_vma=False,
    )
```

```python
import functools
import math

import jax
import jax.numpy as jnp
from jax import lax
from jax.experimental import pallas as pl
from jax.experimental.pallas import tpu as pltpu
from jax.sharding import PartitionSpec as P

HEAD_DIM = 128
MASKED = -1e30
CHUNKS = 5
NT = (((1,), (1,)), ((), ()))
NN = (((1,), (0,)), ((), ()))
BF = jnp.bfloat16
F32 = jnp.float32
VMEM = pl.BlockSpec(memory_space=pltpu.VMEM)
ANYWHERE = pl.BlockSpec(memory_space=pl.ANY)


def dot(a, b, dims=NN):
    return lax.dot_general(a, b, dims, preferred_element_type=F32)


def in_hbm(x):
    return pltpu.with_memory_space_constraint(x, pltpu.HBM)


def position():
    me = lax.axis_index("context").astype(jnp.int32)
    return lax.rem(me, 2), lax.div(me, 2)


def run(moves, sems):
    copies = [pltpu.make_async_copy(a, b, sems.at[i]) for i, (a, b) in enumerate(moves)]
    for copy in copies:
        copy.start()
    return copies


def share_kernel(k, v, q, g, own, theirs, sent, sems):
    core, _ = position()
    moves = []
    for out, owner, left, right in ((theirs, 1 - core, k, v), (own, core, k, v), (sent, 1 - core, q, g)):
        width = out.shape[1] // 2
        cols = pl.ds(pl.multiple_of(owner * width, width), width)
        moves += [
            (left.at[:, cols], out.at[:, pl.ds(0, width)]),
            (right.at[:, cols], out.at[:, pl.ds(width, width)]),
        ]
    for copy in run(moves, sems):
        copy.wait()


def payload_kernel(heads, kv_own, kv_oth, sent_in, sent, *kv):
    core, _ = position()
    rows = kv_own.shape[0]
    width = HEAD_DIM
    for block, part in ((core, kv_own), (1 - core, kv_oth)):
        at = pl.ds(pl.multiple_of(block * rows, rows), rows)
        for s, out in enumerate(kv):
            out[at, :width] = part[:, s * width:(s + 1) * width]
            out[at, width:] = part[:, (heads + s) * width:(heads + s + 1) * width]


def stage_kernel(
    heads, bounds_in, q_all, g_all, other, q_st, g_st, q_t, g_t, k_seg, q_own, g_own, bounds, sems
):
    core, chip = position()
    rows = q_own.shape[0]
    width = HEAD_DIM
    units = q_t.shape[0] // heads
    pairs = units // 2
    two = 2 * rows
    share = q_own.shape[1]
    own = pl.ds(pl.multiple_of(core * share, share), share)
    copies = run([(bounds_in, bounds), (q_all.at[:, own], q_own), (g_all.at[:, own], g_own)], sems)
    copies[0].wait()

    def segment(pos):
        seg = jnp.zeros(pos.shape, jnp.int32)
        for b in range(1, bounds.shape[0] - 1):
            seg += (pos >= bounds[b]).astype(jnp.int32)
        return seg

    sub = lax.broadcasted_iota(jnp.int32, (rows, width), 0)
    seg_lane = lax.broadcasted_iota(jnp.int32, (rows, width), 1)
    for b in range(2 * CHUNKS):
        pos = (2 * (chip + 1 - CHUNKS) + b) * rows + sub
        seg = jnp.where(pos >= 0, segment(pos), width - 1)
        k_seg[b * rows:(b + 1) * rows] = (seg_lane == seg).astype(BF)
    for copy in copies[1:]:
        copy.wait()
    for s in range(heads):
        for p in range(pairs):
            for i in range(2):
                col = ((s * pairs + p) * 2 + i) * width
                cols = slice(col, col + width)
                for block, q, g in ((core, q_own, g_own), (1 - core, other, other.at[:, pl.ds(share, share)])):
                    at = pl.multiple_of((s * units + block * pairs + p) * two + i * rows, rows)
                    q_st[pl.ds(at, rows)] = q[:, cols]
                    g_st[pl.ds(at, rows)] = g[:, cols]
    lane = lax.broadcasted_iota(jnp.int32, (width, two), 1)
    lane = jnp.where(lane >= rows, lane - rows, lane)
    row = lax.broadcasted_iota(jnp.int32, (width, two), 0)
    for block in range(2):
        away = jnp.where(row == segment((2 * chip + block) * rows + lane), 0.0, MASKED).astype(BF)
        for s in range(heads):
            for p in range(pairs):
                u = s * units + block * pairs + p
                q_t[u, :width] = q_st[u * two:(u + 1) * two].T
                q_t[u, width:] = away
                g_t[u] = g_st[u * two:(u + 1) * two].T


def attention_kernel(
    slot, heads, q_st, g_st, q_t, g_t, k_seg, kv4, kv_edge, kv2, kv_middle, kv0, *refs
):
    o_all, dq_all, sent, d4, d_edge, d2, d_middle, d0 = refs[-22:-14]
    (k_aug, v_win, k_t, v_t, qs_st, gs_st, s_scr, p_scr, d_scr, dk_acc, dv_acc, o_scr, dq_scr,
     sems) = refs[-14:]
    width = HEAD_DIM
    scale = width ** -0.5
    core, chip = position()
    units = q_t.shape[0] // heads
    pairs = units // 2
    two = q_t.shape[2]
    rows = two // 2
    wide = 2 * pairs * width
    base = slot * units
    half = pairs * two
    part = (3 * pairs // 2) * two
    sums = ((d_scr, qs_st, dk_acc, scale, 0), (p_scr, gs_st, dv_acc, 1.0, width))
    even = lax.rem(chip, 2) == 0
    edge = pl.multiple_of(jnp.where(even, two, 3 * two), two)
    middle = pl.multiple_of(jnp.where(even, 3 * two, two), two)
    places = [pl.ds(at, two) for at in (0, edge, 2 * two, middle, 4 * two)]

    def attend(blocks):
        whole = blocks == 2 * CHUNKS - 1
        k_aug[:, width:] = k_seg[...]
        for at, kv in zip(places, (kv4, kv_edge, kv2, kv_middle, kv0)):
            k_aug[at, :width] = kv[:, :width]
            v_win[at] = kv[:, width:]
            k_t[:, at] = kv[:, :width].T
            v_t[:width, at] = kv[:, width:].T

        v_t[width:] = jnp.ones((v_t.shape[0] - width, v_t.shape[1]), BF)

        lane = lax.broadcasted_iota(jnp.int32, (rows, two), 1)
        causal = lax.broadcasted_iota(jnp.int32, (rows, two), 0) <= jnp.where(lane >= rows, lane - rows, lane)

        def window(u):
            first = (u // pairs + 2 * CHUNKS - 1 - blocks) * rows
            return first, slice(first, first + blocks * rows)

        def columns(u):
            return slice(u * two, (u + 1) * two)

        def fold(x, op):
            return op(x.reshape(x.shape[0] // 8, 8, x.shape[1]), axis=0)

        def scores(u, top):
            _, keys = window(u)
            s = dot(k_aug[keys], q_t[base + u])
            for b in range(blocks):
                here = slice(b * rows, (b + 1) * rows)
                part = s[here]
                if b == blocks - 1:
                    part = jnp.where(causal, part, MASKED)
                s_scr[u % 2, here] = part
                top = jnp.maximum(top, fold(part, jnp.max))
            return top

        def weights(u, b, peak):
            first, _ = window(u)
            e = jnp.exp2((s_scr[u % 2, b * rows:(b + 1) * rows] - peak) * (scale * math.log2(math.e)))
            p_scr[first + b * rows:first + (b + 1) * rows, columns(u)] = e.astype(BF)

        def score_grads(u, inner):
            _, keys = window(u)
            dp = dot(v_win[keys], g_t[base + u])
            d_scr[keys, columns(u)] = p_scr[keys, columns(u)] * (dp - inner).astype(BF)

        def store(x, out, u):
            block, p = u // pairs, u % pairs
            x = x.T
            for i in range(2):
                out[block * rows:(block + 1) * rows, (2 * p + i) * width:(2 * p + i + 1) * width] = (
                    x[i * rows:(i + 1) * rows]
                )

        def query_grad(u, inv):
            _, keys = window(u)
            store((dot(k_t[:, keys], d_scr[keys, columns(u)]) * (inv * scale)).astype(BF), dq_scr, u)

        first_group = [(b * rows, *one[:3]) for b in range(0, blocks, 3) for one in sums] if whole else []
        second_group = [(rows + b * rows, *one[:3]) for b in range(0, blocks, 3) for one in sums] if whole else []

        def key_grads(turn):
            if turn > pairs and first_group:
                at, left, right, acc = first_group.pop(0)
                at = slice(at, at + 3 * rows)
                acc[at] = dot(left[at, :half], right[:half])
            elif turn > 3 * pairs // 2 and second_group:
                at, left, right, acc = second_group.pop(0)
                at = slice(at, at + 3 * rows)
                acc[at] += dot(left[at, half:part], right[half:part])

        def outputs(u):
            _, keys = window(u)
            o = dot(v_t[:, keys], p_scr[keys, columns(u)])
            inv = 1.0 / o[width:width + 1]
            o = (o[:width] * inv).astype(BF)
            store(o, o_scr, u)
            inner = jnp.sum(g_t[base + u].astype(F32) * o.astype(F32), axis=0, keepdims=True)
            column = jnp.broadcast_to(inv, (8, two)).T[:, :1]
            here, there = slice(u * two, (u + 1) * two), slice((base + u) * two, (base + u + 1) * two)
            qs_st[here] = (q_st[there].astype(F32) * column).astype(BF)
            gs_st[here] = (g_st[there].astype(F32) * column).astype(BF)
            return inv, inner

        def turn(u, peak, inv, inner):
            top = jnp.full((8, two), MASKED, F32)
            if u + 1 < units:
                top = scores(u + 1, top)
            key_grads(u)
            if 0 <= u < units:
                for b in range(blocks):
                    weights(u, b, peak)
                    if b % 3 == 2:
                        key_grads(u)
            if u > 0:
                score_grads(u - 1, inner)
            if u + 1 >= units:
                key_grads(u)
                key_grads(u)
            if u > 0:
                query_grad(u - 1, inv)
            if 0 <= u < units:
                inv, inner = outputs(u)
            return jnp.max(top, axis=0, keepdims=True), inv, inner

        if whole:
            for one in sums:
                one[2][blocks * rows:] = jnp.zeros((rows, width), F32)
        state = (None, None, None)
        for u in range(-1, units + 1):
            state = turn(u, *state)

        mine = pl.ds(pl.multiple_of(core * rows, rows), rows)
        other = pl.ds(pl.multiple_of((1 - core) * rows, rows), rows)
        cols = pl.ds(pl.multiple_of((core * heads + slot) * wide, wide), wide)
        moves = [
            (o_scr.at[other], sent.at[:, pl.ds(0, wide)]),
            (dq_scr.at[other], sent.at[:, pl.ds(wide, wide)]),
            (o_scr.at[mine], o_all.at[:, cols]),
            (dq_scr.at[mine], dq_all.at[:, cols]),
        ]
        copies = run(moves, sems)

        for left, right, acc, factor, col in sums:
            cols = slice(col, col + width)
            late = 3 * two
            if whole:
                acc[rows:] += dot(left[rows:, part:], right[part:])
            else:
                acc[:late] = jnp.zeros((late, width), F32)
                acc[late:] = dot(left[late:, half:], right[half:])
                acc[late:late + 3 * rows] += dot(left[late:late + 3 * rows, :half], right[:half])
            for at, out in zip(places, (d4, d_edge, d2, d_middle, d0)):
                out[:, cols] = (factor * acc[at]).astype(out.dtype)
        for copy in copies:
            copy.wait()

    @pl.when(chip >= 2)
    def _():
        attend(2 * CHUNKS - 1)

    @pl.when(chip < 2)
    def _():
        attend(4)


def place_kernel(heads, o_in, dq_in, *refs):
    backs = refs[:heads]
    mine, theirs, o, dq, dk, dv, sems = refs[heads:]
    core, _ = position()
    wide = backs[0].shape[1] // 2
    half = mine.shape[1] // 2
    moves = []
    for s, back in enumerate(backs):
        cols = pl.ds(pl.multiple_of(((1 - core) * heads + s) * wide, wide), wide)
        moves += [(back.at[:, pl.ds(0, wide)], o.at[:, cols]), (back.at[:, pl.ds(wide, wide)], dq.at[:, cols])]
    for part, owner in ((mine, core), (theirs, 1 - core)):
        cols = pl.ds(pl.multiple_of(owner * half, half), half)
        moves += [(part.at[:, pl.ds(0, half)], dk.at[:, cols]), (part.at[:, pl.ds(half, half)], dv.at[:, cols])]
    for copy in run(moves, sems):
        copy.wait()


def shares(k, v, q, g):
    return pl.pallas_call(
        share_kernel,
        in_specs=[ANYWHERE] * 4,
        out_specs=[VMEM] * 3,
        out_shape=[jax.ShapeDtypeStruct(x.shape, BF) for x in (k, v, q)],
        scratch_shapes=[pltpu.SemaphoreType.DMA((6,))],
        compiler_params=pltpu.CompilerParams(vmem_limit_bytes=4 * 1024 * 1024),
        name="share",
    )(in_hbm(k), in_hbm(v), in_hbm(q), in_hbm(g))


def payloads(kv_own, kv_oth, sent, heads):
    kv = jax.ShapeDtypeStruct((2 * kv_own.shape[0], 2 * HEAD_DIM), BF)
    return pl.pallas_call(
        functools.partial(payload_kernel, heads),
        in_specs=[VMEM] * 2 + [ANYWHERE],
        out_specs=[ANYWHERE] + [VMEM] * heads,
        out_shape=[jax.ShapeDtypeStruct(sent.shape, BF)] + [kv] * heads,
        input_output_aliases={2: 0},
        compiler_params=pltpu.CompilerParams(vmem_limit_bytes=4 * 1024 * 1024),
        name="payload",
    )(kv_own, kv_oth, sent)


def staged(bounds, q, g, other, heads):
    rows = q.shape[0]
    width = HEAD_DIM
    units = q.shape[1] // (2 * width)
    return pl.pallas_call(
        functools.partial(stage_kernel, heads),
        in_specs=[ANYWHERE, ANYWHERE, ANYWHERE, VMEM],
        out_specs=[VMEM] * 5,
        out_shape=[
            jax.ShapeDtypeStruct((units * 2 * rows, width), BF),
            jax.ShapeDtypeStruct((units * 2 * rows, width), BF),
            jax.ShapeDtypeStruct((units, 2 * width, 2 * rows), BF),
            jax.ShapeDtypeStruct((units, width, 2 * rows), BF),
            jax.ShapeDtypeStruct((2 * CHUNKS * rows, width), BF),
        ],
        scratch_shapes=[
            pltpu.VMEM((rows, q.shape[1] // 2), BF),
            pltpu.VMEM((rows, q.shape[1] // 2), BF),
            pltpu.SMEM(bounds.shape, jnp.int32),
            pltpu.SemaphoreType.DMA((3,)),
        ],
        compiler_params=pltpu.CompilerParams(vmem_limit_bytes=16 * 1024 * 1024),
        cost_estimate=pl.CostEstimate(flops=0, bytes_accessed=8 * q.size, transcendentals=0),
        name="stage",
    )(in_hbm(bounds), in_hbm(q), in_hbm(g), other)


def head_attention(slot, heads, q, stage, window, so_far):
    rows = q.shape[0]
    width = HEAD_DIM
    two = 2 * rows
    units = stage[2].shape[0] // heads
    wide = q.shape[1] // (2 * heads)
    span = CHUNKS * two
    short = span - rows
    chunk = window[0].shape
    return pl.pallas_call(
        functools.partial(attention_kernel, slot, heads),
        in_specs=[VMEM] * 10 + [ANYWHERE] * len(so_far),
        out_specs=[ANYWHERE] * 3 + [VMEM] * 5,
        scratch_shapes=[
            pltpu.VMEM((span, 2 * width), BF),
            pltpu.VMEM((span, width), BF),
            pltpu.VMEM((width, span), BF),
            pltpu.VMEM((width + 16, span), BF),
            pltpu.VMEM((units * two, width), BF),
            pltpu.VMEM((units * two, width), BF),
            pltpu.VMEM((2, short, two), F32),
            pltpu.VMEM((span, units * two), BF),
            pltpu.VMEM((span, units * two), BF),
            pltpu.VMEM((span, width), F32),
            pltpu.VMEM((span, width), F32),
            pltpu.VMEM((two, wide), BF),
            pltpu.VMEM((two, wide), BF),
            pltpu.SemaphoreType.DMA((4,)),
        ],
        out_shape=[
            jax.ShapeDtypeStruct(q.shape, BF),
            jax.ShapeDtypeStruct(q.shape, BF),
            jax.ShapeDtypeStruct((rows, 2 * wide), BF),
        ] + [jax.ShapeDtypeStruct(chunk, t) for t in (BF, BF, F32, BF, F32)],
        input_output_aliases={10 + i: i for i in range(len(so_far))},
        compiler_params=pltpu.CompilerParams(vmem_limit_bytes=36 * 1024 * 1024),
        cost_estimate=pl.CostEstimate(
            flops=20 * rows * span * wide,
            bytes_accessed=24 * rows * wide,
            transcendentals=2 * rows * span * wide // width,
        ),
        name="attention%d" % slot,
    )(*stage, *window, *so_far)


def place(o, dq, backs, mine, theirs):
    heads = len(backs)
    return pl.pallas_call(
        functools.partial(place_kernel, heads),
        in_specs=[ANYWHERE] * (4 + heads),
        out_specs=[ANYWHERE] * 4,
        scratch_shapes=[pltpu.SemaphoreType.DMA((2 * heads + 4,))],
        out_shape=[
            jax.ShapeDtypeStruct(o.shape, BF),
            jax.ShapeDtypeStruct(dq.shape, BF),
            jax.ShapeDtypeStruct(mine.shape, BF),
            jax.ShapeDtypeStruct(mine.shape, BF),
        ],
        input_output_aliases={0: 0, 1: 1},
        compiler_params=pltpu.CompilerParams(vmem_limit_bytes=1024 * 1024),
        name="place",
    )(o, dq, *backs, mine, theirs)


def body(query_rows, key_rows, value_rows, grad_out, doc_bounds):
    core, chip = position()
    n = lax.axis_size("context")
    even = lax.rem(chip, 2) == 0
    rows = query_rows.shape[0]
    width = HEAD_DIM
    heads = key_rows.shape[1] // (2 * width)

    def shift(x, by):
        return lax.ppermute(x, "context", [(i, (i + by) % n) for i in range(n)])

    def swap(x):
        return lax.ppermute(x, "context", [(i, i ^ 1) for i in range(n)])

    def across(x):
        return lax.ppermute(x, "context", [(i, i ^ 2) for i in range(n)])

    kv_own, kv_sent, sent = shares(key_rows, value_rows, query_rows, grad_out)
    sent, *kv = payloads(kv_own, swap(kv_sent), sent, heads)
    stage = staged(doc_bounds, query_rows, grad_out, swap(sent), heads)

    o, dq, outs = None, None, []
    for s in range(heads):
        back2 = shift(kv[s], 4)
        edge = shift(jnp.where(even, kv[s], back2), 2)
        middle = across(back2)
        back4 = shift(back2, 4)
        o, dq, *rest = head_attention(
            s, heads, query_rows, stage, (back4, edge, back2, middle, kv[s]), () if s == 0 else (o, dq)
        )
        outs.append(rest)
    grads, backs = [], []
    for sent, d4, d_edge, d2, d_middle, d0 in outs:
        from_edge = shift(d_edge, -2)
        from_four = shift(d4, -4)
        from_middle = across(d_middle)
        d2 = jnp.where(even, d2, d2 + from_edge)
        from_two = shift((d2 + from_middle + from_four).astype(BF), -4)
        total = jnp.where(even, d0 + from_edge, d0) + from_two.astype(F32)
        grads.append(total.astype(BF))
        backs.append(swap(sent))
    total = jnp.concatenate([g[:, :width] for g in grads] + [g[:, width:] for g in grads], axis=1)
    mine = lax.dynamic_slice_in_dim(total, core * rows, rows, 0)
    theirs = swap(lax.dynamic_slice_in_dim(total, (1 - core) * rows, rows, 0))
    return place(o, dq, backs, mine, theirs)


def solution(mesh):
    rows = P(("dp", "context"), None)
    return jax.shard_map(
        body,
        mesh=mesh,
        in_specs=(rows, rows, rows, rows, P("dp")),
        out_specs=(rows, rows, rows, rows),
        check_vma=False,
    )
```

```python
import functools
import math

import jax
import jax.numpy as jnp
from jax import lax
from jax.experimental import pallas as pl
from jax.experimental.pallas import tpu as pltpu
from jax.sharding import PartitionSpec as P

HEAD_DIM = 128
MASKED = -1e30
CHUNKS = 5
NT = (((1,), (1,)), ((), ()))
NN = (((1,), (0,)), ((), ()))
BF = jnp.bfloat16
F32 = jnp.float32
VMEM = pl.BlockSpec(memory_space=pltpu.VMEM)
ANYWHERE = pl.BlockSpec(memory_space=pl.ANY)


def dot(a, b, dims=NN):
    return lax.dot_general(a, b, dims, preferred_element_type=F32)


def in_hbm(x):
    return pltpu.with_memory_space_constraint(x, pltpu.HBM)


def position():
    me = lax.axis_index("context").astype(jnp.int32)
    return lax.rem(me, 2), lax.div(me, 2)


def run(moves, sems):
    copies = [pltpu.make_async_copy(a, b, sems.at[i]) for i, (a, b) in enumerate(moves)]
    for copy in copies:
        copy.start()
    return copies


def share_kernel(k, v, q, g, own, theirs, sent, sems):
    core, _ = position()
    moves = []
    for out, owner, left, right in ((theirs, 1 - core, k, v), (own, core, k, v), (sent, 1 - core, q, g)):
        width = out.shape[1] // 2
        cols = pl.ds(pl.multiple_of(owner * width, width), width)
        moves += [
            (left.at[:, cols], out.at[:, pl.ds(0, width)]),
            (right.at[:, cols], out.at[:, pl.ds(width, width)]),
        ]
    for copy in run(moves, sems):
        copy.wait()


def payload_kernel(heads, kv_own, kv_oth, sent_in, sent, *kv):
    core, _ = position()
    rows = kv_own.shape[0]
    width = HEAD_DIM
    for block, part in ((core, kv_own), (1 - core, kv_oth)):
        at = pl.ds(pl.multiple_of(block * rows, rows), rows)
        for s, out in enumerate(kv):
            out[at, :width] = part[:, s * width:(s + 1) * width]
            out[at, width:] = part[:, (heads + s) * width:(heads + s + 1) * width]


def stage_kernel(
    heads, bounds_in, q_all, g_all, other, q_st, g_st, q_t, g_t, k_seg, q_own, g_own, bounds, sems
):
    core, chip = position()
    rows = q_own.shape[0]
    width = HEAD_DIM
    units = q_t.shape[0] // heads
    pairs = units // 2
    two = 2 * rows
    share = q_own.shape[1]
    own = pl.ds(pl.multiple_of(core * share, share), share)
    copies = run([(bounds_in, bounds), (q_all.at[:, own], q_own), (g_all.at[:, own], g_own)], sems)
    copies[0].wait()

    def segment(pos):
        seg = jnp.zeros(pos.shape, jnp.int32)
        for b in range(1, bounds.shape[0] - 1):
            seg += (pos >= bounds[b]).astype(jnp.int32)
        return seg

    sub = lax.broadcasted_iota(jnp.int32, (rows, width), 0)
    seg_lane = lax.broadcasted_iota(jnp.int32, (rows, width), 1)
    for b in range(2 * CHUNKS):
        pos = (2 * (chip + 1 - CHUNKS) + b) * rows + sub
        seg = jnp.where(pos >= 0, segment(pos), width - 1)
        k_seg[b * rows:(b + 1) * rows] = (seg_lane == seg).astype(BF)
    for copy in copies[1:]:
        copy.wait()
    for s in range(heads):
        for p in range(pairs):
            for i in range(2):
                col = ((s * pairs + p) * 2 + i) * width
                cols = slice(col, col + width)
                for block, q, g in ((core, q_own, g_own), (1 - core, other, other.at[:, pl.ds(share, share)])):
                    at = pl.multiple_of((s * units + block * pairs + p) * two + i * rows, rows)
                    q_st[pl.ds(at, rows)] = q[:, cols]
                    g_st[pl.ds(at, rows)] = g[:, cols]
    lane = lax.broadcasted_iota(jnp.int32, (width, two), 1)
    lane = jnp.where(lane >= rows, lane - rows, lane)
    row = lax.broadcasted_iota(jnp.int32, (width, two), 0)
    for block in range(2):
        away = jnp.where(row == segment((2 * chip + block) * rows + lane), 0.0, MASKED).astype(BF)
        for s in range(heads):
            for p in range(pairs):
                u = s * units + block * pairs + p
                q_t[u, :width] = q_st[u * two:(u + 1) * two].T
                q_t[u, width:] = away
                g_t[u] = g_st[u * two:(u + 1) * two].T


def attention_kernel(
    slot, heads, q_st, g_st, q_t, g_t, k_seg, kv4, kv_edge, kv2, kv_middle, kv0, *refs
):
    o_all, dq_all, sent, d4, d_edge, d2, d_middle, d0 = refs[-22:-14]
    (k_aug, v_win, k_t, v_t, qs_st, gs_st, s_scr, p_scr, d_scr, dk_acc, dv_acc, o_scr, dq_scr,
     sems) = refs[-14:]
    width = HEAD_DIM
    scale = width ** -0.5
    core, chip = position()
    units = q_t.shape[0] // heads
    pairs = units // 2
    two = q_t.shape[2]
    rows = two // 2
    wide = 2 * pairs * width
    base = slot * units
    half = pairs * two
    part = (3 * pairs // 2) * two
    sums = ((d_scr, qs_st, dk_acc, scale, 0), (p_scr, gs_st, dv_acc, 1.0, width))
    even = lax.rem(chip, 2) == 0
    edge = pl.multiple_of(jnp.where(even, two, 3 * two), two)
    middle = pl.multiple_of(jnp.where(even, 3 * two, two), two)
    places = [pl.ds(at, two) for at in (0, edge, 2 * two, middle, 4 * two)]

    def attend(blocks, step):
        whole = blocks == 2 * CHUNKS - 1
        k_aug[:, width:] = k_seg[...]
        for at, kv in zip(places, (kv4, kv_edge, kv2, kv_middle, kv0)):
            k_aug[at, :width] = kv[:, :width]
            v_win[at] = kv[:, width:]
            k_t[:, at] = kv[:, :width].T
            v_t[:width, at] = kv[:, width:].T

        v_t[width:] = jnp.ones((v_t.shape[0] - width, v_t.shape[1]), BF)

        lane = lax.broadcasted_iota(jnp.int32, (rows, two), 1)
        causal = lax.broadcasted_iota(jnp.int32, (rows, two), 0) <= jnp.where(lane >= rows, lane - rows, lane)

        def window(u):
            first = (u // pairs + 2 * CHUNKS - 1 - blocks) * rows
            return first, slice(first, first + blocks * rows)

        def columns(u):
            return slice(u * two, (u + 1) * two)

        def fold(x, op):
            return op(x.reshape(x.shape[0] // 8, 8, x.shape[1]), axis=0)

        def scores(u, b, top):
            first, _ = window(u)
            s = dot(k_aug[first + b * rows:first + (b + step) * rows], q_t[base + u])
            for i in range(step):
                part = s[i * rows:(i + 1) * rows]
                if b + i == blocks - 1:
                    part = jnp.where(causal, part, MASKED)
                s_scr[u % 2, (b + i) * rows:(b + i + 1) * rows] = part
                top = jnp.maximum(top, fold(part, jnp.max))
            return top

        def weights(u, b, peak):
            first, _ = window(u)
            e = jnp.exp2((s_scr[u % 2, b * rows:(b + 1) * rows] - peak) * (scale * math.log2(math.e)))
            p_scr[first + b * rows:first + (b + 1) * rows, columns(u)] = e.astype(BF)

        def score_grads(u, b, inner):
            first, _ = window(u)
            keys = slice(first + b * rows, first + (b + step) * rows)
            dp = dot(v_win[keys], g_t[base + u])
            d_scr[keys, columns(u)] = p_scr[keys, columns(u)] * (dp - inner).astype(BF)

        def store(x, out, u):
            block, p = u // pairs, u % pairs
            x = x.T
            for i in range(2):
                out[block * rows:(block + 1) * rows, (2 * p + i) * width:(2 * p + i + 1) * width] = (
                    x[i * rows:(i + 1) * rows]
                )

        def query_grad(u, inv):
            _, keys = window(u)
            store((dot(k_t[:, keys], d_scr[keys, columns(u)]) * (inv * scale)).astype(BF), dq_scr, u)

        first_group = [(b * rows, *one[:3]) for b in range(0, blocks, 3) for one in sums] if whole else []
        second_group = [(rows + b * rows, *one[:3]) for b in range(0, blocks, 3) for one in sums] if whole else []

        def key_grads(turn):
            if turn > pairs and first_group:
                at, left, right, acc = first_group.pop(0)
                at = slice(at, at + 3 * rows)
                acc[at] = dot(left[at, :half], right[:half])
            elif turn > 3 * pairs // 2 and second_group:
                at, left, right, acc = second_group.pop(0)
                at = slice(at, at + 3 * rows)
                acc[at] += dot(left[at, half:part], right[half:part])

        def outputs(u):
            _, keys = window(u)
            o = dot(v_t[:, keys], p_scr[keys, columns(u)])
            inv = 1.0 / o[width:width + 1]
            o = (o[:width] * inv).astype(BF)
            store(o, o_scr, u)
            inner = jnp.sum(g_t[base + u].astype(F32) * o.astype(F32), axis=0, keepdims=True)
            column = jnp.broadcast_to(inv, (8, two)).T[:, :1]
            here, there = slice(u * two, (u + 1) * two), slice((base + u) * two, (base + u + 1) * two)
            qs_st[here] = (q_st[there].astype(F32) * column).astype(BF)
            gs_st[here] = (g_st[there].astype(F32) * column).astype(BF)
            return inv, inner

        def turn(u, peak, inv, inner):
            top = jnp.full((8, two), MASKED, F32)
            for b in range(0, blocks, step):
                if u + 1 < units:
                    top = scores(u + 1, b, top)
                if 0 <= u < units:
                    for i in range(step):
                        weights(u, b + i, peak)
                if u > 0:
                    score_grads(u - 1, b, inner)
                if b % 3 == 0:
                    key_grads(u)
                    if u + 1 >= units:
                        key_grads(u)
            if u > 0:
                query_grad(u - 1, inv)
            if 0 <= u < units:
                inv, inner = outputs(u)
            return jnp.max(top, axis=0, keepdims=True), inv, inner

        if whole:
            for one in sums:
                one[2][blocks * rows:] = jnp.zeros((rows, width), F32)
        state = (None, None, None)
        for u in range(-1, units + 1):
            state = turn(u, *state)

        mine = pl.ds(pl.multiple_of(core * rows, rows), rows)
        other = pl.ds(pl.multiple_of((1 - core) * rows, rows), rows)
        cols = pl.ds(pl.multiple_of((core * heads + slot) * wide, wide), wide)
        moves = [
            (o_scr.at[other], sent.at[:, pl.ds(0, wide)]),
            (dq_scr.at[other], sent.at[:, pl.ds(wide, wide)]),
            (o_scr.at[mine], o_all.at[:, cols]),
            (dq_scr.at[mine], dq_all.at[:, cols]),
        ]
        copies = run(moves, sems)

        for left, right, acc, factor, col in sums:
            cols = slice(col, col + width)
            late = 3 * two
            if not whole:
                acc[:late] = jnp.zeros((late, width), F32)
                acc[late:] = dot(left[late:, half:], right[half:])
                acc[late:late + 3 * rows] += dot(left[late:late + 3 * rows, :half], right[:half])

            def total(keys):
                return factor * (acc[keys] + dot(left[keys, part:], right[part:]) if whole else acc[keys])

            d4[:rows, cols] = (factor * acc[:rows]).astype(d4.dtype)
            d4[rows:, cols] = total(slice(rows, two)).astype(d4.dtype)
            for at, out in zip(places[1:], (d_edge, d2, d_middle, d0)):
                out[:, cols] = total(at).astype(out.dtype)
        for copy in copies:
            copy.wait()

    @pl.when(chip >= 2)
    def _():
        attend(2 * CHUNKS - 1, 1)

    @pl.when(chip < 2)
    def _():
        attend(4, 1)


def place_kernel(heads, o_in, dq_in, *refs):
    backs = refs[:heads]
    mine, theirs, o, dq, dk, dv, sems = refs[heads:]
    core, _ = position()
    wide = backs[0].shape[1] // 2
    half = mine.shape[1] // 2
    moves = []
    for s, back in enumerate(backs):
        cols = pl.ds(pl.multiple_of(((1 - core) * heads + s) * wide, wide), wide)
        moves += [(back.at[:, pl.ds(0, wide)], o.at[:, cols]), (back.at[:, pl.ds(wide, wide)], dq.at[:, cols])]
    for part, owner in ((mine, core), (theirs, 1 - core)):
        cols = pl.ds(pl.multiple_of(owner * half, half), half)
        moves += [(part.at[:, pl.ds(0, half)], dk.at[:, cols]), (part.at[:, pl.ds(half, half)], dv.at[:, cols])]
    for copy in run(moves, sems):
        copy.wait()


def shares(k, v, q, g):
    return pl.pallas_call(
        share_kernel,
        in_specs=[ANYWHERE] * 4,
        out_specs=[VMEM] * 3,
        out_shape=[jax.ShapeDtypeStruct(x.shape, BF) for x in (k, v, q)],
        scratch_shapes=[pltpu.SemaphoreType.DMA((6,))],
        compiler_params=pltpu.CompilerParams(vmem_limit_bytes=4 * 1024 * 1024),
        name="share",
    )(in_hbm(k), in_hbm(v), in_hbm(q), in_hbm(g))


def payloads(kv_own, kv_oth, sent, heads):
    kv = jax.ShapeDtypeStruct((2 * kv_own.shape[0], 2 * HEAD_DIM), BF)
    return pl.pallas_call(
        functools.partial(payload_kernel, heads),
        in_specs=[VMEM] * 2 + [ANYWHERE],
        out_specs=[ANYWHERE] + [VMEM] * heads,
        out_shape=[jax.ShapeDtypeStruct(sent.shape, BF)] + [kv] * heads,
        input_output_aliases={2: 0},
        compiler_params=pltpu.CompilerParams(vmem_limit_bytes=4 * 1024 * 1024),
        name="payload",
    )(kv_own, kv_oth, sent)


def staged(bounds, q, g, other, heads):
    rows = q.shape[0]
    width = HEAD_DIM
    units = q.shape[1] // (2 * width)
    return pl.pallas_call(
        functools.partial(stage_kernel, heads),
        in_specs=[ANYWHERE, ANYWHERE, ANYWHERE, VMEM],
        out_specs=[VMEM] * 5,
        out_shape=[
            jax.ShapeDtypeStruct((units * 2 * rows, width), BF),
            jax.ShapeDtypeStruct((units * 2 * rows, width), BF),
            jax.ShapeDtypeStruct((units, 2 * width, 2 * rows), BF),
            jax.ShapeDtypeStruct((units, width, 2 * rows), BF),
            jax.ShapeDtypeStruct((2 * CHUNKS * rows, width), BF),
        ],
        scratch_shapes=[
            pltpu.VMEM((rows, q.shape[1] // 2), BF),
            pltpu.VMEM((rows, q.shape[1] // 2), BF),
            pltpu.SMEM(bounds.shape, jnp.int32),
            pltpu.SemaphoreType.DMA((3,)),
        ],
        compiler_params=pltpu.CompilerParams(vmem_limit_bytes=16 * 1024 * 1024),
        cost_estimate=pl.CostEstimate(flops=0, bytes_accessed=8 * q.size, transcendentals=0),
        name="stage",
    )(in_hbm(bounds), in_hbm(q), in_hbm(g), other)


def head_attention(slot, heads, q, stage, window, so_far):
    rows = q.shape[0]
    width = HEAD_DIM
    two = 2 * rows
    units = stage[2].shape[0] // heads
    wide = q.shape[1] // (2 * heads)
    span = CHUNKS * two
    short = span - rows
    chunk = window[0].shape
    return pl.pallas_call(
        functools.partial(attention_kernel, slot, heads),
        in_specs=[VMEM] * 10 + [ANYWHERE] * len(so_far),
        out_specs=[ANYWHERE] * 3 + [VMEM] * 5,
        scratch_shapes=[
            pltpu.VMEM((span, 2 * width), BF),
            pltpu.VMEM((span, width), BF),
            pltpu.VMEM((width, span), BF),
            pltpu.VMEM((width + 16, span), BF),
            pltpu.VMEM((units * two, width), BF),
            pltpu.VMEM((units * two, width), BF),
            pltpu.VMEM((2, short, two), F32),
            pltpu.VMEM((span, units * two), BF),
            pltpu.VMEM((span, units * two), BF),
            pltpu.VMEM((span, width), F32),
            pltpu.VMEM((span, width), F32),
            pltpu.VMEM((two, wide), BF),
            pltpu.VMEM((two, wide), BF),
            pltpu.SemaphoreType.DMA((4,)),
        ],
        out_shape=[
            jax.ShapeDtypeStruct(q.shape, BF),
            jax.ShapeDtypeStruct(q.shape, BF),
            jax.ShapeDtypeStruct((rows, 2 * wide), BF),
        ] + [jax.ShapeDtypeStruct(chunk, t) for t in (BF, BF, F32, BF, F32)],
        input_output_aliases={10 + i: i for i in range(len(so_far))},
        compiler_params=pltpu.CompilerParams(vmem_limit_bytes=36 * 1024 * 1024),
        cost_estimate=pl.CostEstimate(
            flops=20 * rows * span * wide,
            bytes_accessed=24 * rows * wide,
            transcendentals=2 * rows * span * wide // width,
        ),
        name="attention%d" % slot,
    )(*stage, *window, *so_far)


def place(o, dq, backs, mine, theirs):
    heads = len(backs)
    return pl.pallas_call(
        functools.partial(place_kernel, heads),
        in_specs=[ANYWHERE] * (4 + heads),
        out_specs=[ANYWHERE] * 4,
        scratch_shapes=[pltpu.SemaphoreType.DMA((2 * heads + 4,))],
        out_shape=[
            jax.ShapeDtypeStruct(o.shape, BF),
            jax.ShapeDtypeStruct(dq.shape, BF),
            jax.ShapeDtypeStruct(mine.shape, BF),
            jax.ShapeDtypeStruct(mine.shape, BF),
        ],
        input_output_aliases={0: 0, 1: 1},
        compiler_params=pltpu.CompilerParams(vmem_limit_bytes=1024 * 1024),
        name="place",
    )(o, dq, *backs, mine, theirs)


def body(query_rows, key_rows, value_rows, grad_out, doc_bounds):
    core, chip = position()
    n = lax.axis_size("context")
    even = lax.rem(chip, 2) == 0
    rows = query_rows.shape[0]
    width = HEAD_DIM
    heads = key_rows.shape[1] // (2 * width)

    def shift(x, by):
        return lax.ppermute(x, "context", [(i, (i + by) % n) for i in range(n)])

    def swap(x):
        return lax.ppermute(x, "context", [(i, i ^ 1) for i in range(n)])

    def across(x):
        return lax.ppermute(x, "context", [(i, i ^ 2) for i in range(n)])

    kv_own, kv_sent, sent = shares(key_rows, value_rows, query_rows, grad_out)
    sent, *kv = payloads(kv_own, swap(kv_sent), sent, heads)
    stage = staged(doc_bounds, query_rows, grad_out, swap(sent), heads)

    o, dq, outs = None, None, []
    for s in range(heads):
        back2 = shift(kv[s], 4)
        edge = shift(jnp.where(even, kv[s], back2), 2)
        middle = across(back2)
        back4 = shift(back2, 4)
        o, dq, *rest = head_attention(
            s, heads, query_rows, stage, (back4, edge, back2, middle, kv[s]), () if s == 0 else (o, dq)
        )
        outs.append(rest)
    grads, backs = [], []
    for sent, d4, d_edge, d2, d_middle, d0 in outs:
        from_edge = shift(d_edge, -2)
        from_four = shift(d4, -4)
        from_middle = across(d_middle)
        d2 = jnp.where(even, d2, d2 + from_edge)
        from_two = shift((d2 + from_middle + from_four).astype(BF), -4)
        total = jnp.where(even, d0 + from_edge, d0) + from_two.astype(F32)
        grads.append(total.astype(BF))
        backs.append(swap(sent))
    total = jnp.concatenate([g[:, :width] for g in grads] + [g[:, width:] for g in grads], axis=1)
    mine = lax.dynamic_slice_in_dim(total, core * rows, rows, 0)
    theirs = swap(lax.dynamic_slice_in_dim(total, (1 - core) * rows, rows, 0))
    return place(o, dq, backs, mine, theirs)


def solution(mesh):
    rows = P(("dp", "context"), None)
    return jax.shard_map(
        body,
        mesh=mesh,
        in_specs=(rows, rows, rows, rows, P("dp")),
        out_specs=(rows, rows, rows, rows),
        check_vma=False,
    )
```

```python
import functools
import math

import jax
import jax.numpy as jnp
from jax import lax
from jax.experimental import pallas as pl
from jax.experimental.pallas import tpu as pltpu
from jax.sharding import PartitionSpec as P

HEAD_DIM = 128
MASKED = -1e30
CHUNKS = 5
NT = (((1,), (1,)), ((), ()))
NN = (((1,), (0,)), ((), ()))
BF = jnp.bfloat16
F32 = jnp.float32
VMEM = pl.BlockSpec(memory_space=pltpu.VMEM)
ANYWHERE = pl.BlockSpec(memory_space=pl.ANY)


def dot(a, b, dims=NN):
    return lax.dot_general(a, b, dims, preferred_element_type=F32)


def in_hbm(x):
    return pltpu.with_memory_space_constraint(x, pltpu.HBM)


def position():
    me = lax.axis_index("context").astype(jnp.int32)
    return lax.rem(me, 2), lax.div(me, 2)


def run(moves, sems):
    copies = [pltpu.make_async_copy(a, b, sems.at[i]) for i, (a, b) in enumerate(moves)]
    for copy in copies:
        copy.start()
    return copies


def share_kernel(k, v, q, g, own, theirs, sent, sems):
    core, _ = position()
    moves = []
    for out, owner, left, right in ((theirs, 1 - core, k, v), (own, core, k, v), (sent, 1 - core, q, g)):
        width = out.shape[1] // 2
        cols = pl.ds(pl.multiple_of(owner * width, width), width)
        moves += [
            (left.at[:, cols], out.at[:, pl.ds(0, width)]),
            (right.at[:, cols], out.at[:, pl.ds(width, width)]),
        ]
    for copy in run(moves, sems):
        copy.wait()


def payload_kernel(heads, kv_own, kv_oth, sent_in, sent, *kv):
    core, _ = position()
    rows = kv_own.shape[0]
    width = HEAD_DIM
    for block, part in ((core, kv_own), (1 - core, kv_oth)):
        at = pl.ds(pl.multiple_of(block * rows, rows), rows)
        for s, out in enumerate(kv):
            out[at, :width] = part[:, s * width:(s + 1) * width]
            out[at, width:] = part[:, (heads + s) * width:(heads + s + 1) * width]


def stage_kernel(
    heads, bounds_in, q_all, g_all, other, q_st, g_st, q_t, g_t, k_seg, q_own, g_own, bounds, sems
):
    core, chip = position()
    rows = q_own.shape[0]
    width = HEAD_DIM
    units = q_t.shape[0] // heads
    pairs = units // 2
    two = 2 * rows
    share = q_own.shape[1]
    own = pl.ds(pl.multiple_of(core * share, share), share)
    copies = run([(bounds_in, bounds), (q_all.at[:, own], q_own), (g_all.at[:, own], g_own)], sems)
    copies[0].wait()

    def segment(pos):
        seg = jnp.zeros(pos.shape, jnp.int32)
        for b in range(1, bounds.shape[0] - 1):
            seg += (pos >= bounds[b]).astype(jnp.int32)
        return seg

    sub = lax.broadcasted_iota(jnp.int32, (rows, width), 0)
    seg_lane = lax.broadcasted_iota(jnp.int32, (rows, width), 1)
    for b in range(2 * CHUNKS):
        pos = (2 * (chip + 1 - CHUNKS) + b) * rows + sub
        seg = jnp.where(pos >= 0, segment(pos), width - 1)
        k_seg[b * rows:(b + 1) * rows] = (seg_lane == seg).astype(BF)
    for copy in copies[1:]:
        copy.wait()
    for s in range(heads):
        for p in range(pairs):
            for i in range(2):
                col = ((s * pairs + p) * 2 + i) * width
                cols = slice(col, col + width)
                for block, q, g in ((core, q_own, g_own), (1 - core, other, other.at[:, pl.ds(share, share)])):
                    at = pl.multiple_of((s * units + block * pairs + p) * two + i * rows, rows)
                    q_st[pl.ds(at, rows)] = q[:, cols]
                    g_st[pl.ds(at, rows)] = g[:, cols]
    lane = lax.broadcasted_iota(jnp.int32, (width, two), 1)
    lane = jnp.where(lane >= rows, lane - rows, lane)
    row = lax.broadcasted_iota(jnp.int32, (width, two), 0)
    for block in range(2):
        away = jnp.where(row == segment((2 * chip + block) * rows + lane), 0.0, MASKED).astype(BF)
        for s in range(heads):
            for p in range(pairs):
                u = s * units + block * pairs + p
                q_t[u, :width] = q_st[u * two:(u + 1) * two].T
                q_t[u, width:] = away
                g_t[u] = g_st[u * two:(u + 1) * two].T


def attention_kernel(
    slot, heads, q_st, g_st, q_t, g_t, k_seg, kv4, kv_edge, kv2, kv_middle, kv0, *refs
):
    o_all, dq_all, sent, d4, d_edge, d2, d_middle, d0 = refs[-22:-14]
    (k_aug, v_win, k_t, v_t, qs_st, gs_st, s_scr, p_scr, d_scr, dk_acc, dv_acc, o_scr, dq_scr,
     sems) = refs[-14:]
    width = HEAD_DIM
    scale = width ** -0.5
    core, chip = position()
    units = q_t.shape[0] // heads
    pairs = units // 2
    two = q_t.shape[2]
    rows = two // 2
    wide = 2 * pairs * width
    base = slot * units
    half = pairs * two
    part = (3 * pairs // 2) * two
    sums = ((d_scr, qs_st, dk_acc, scale, 0), (p_scr, gs_st, dv_acc, 1.0, width))
    even = lax.rem(chip, 2) == 0
    edge = pl.multiple_of(jnp.where(even, two, 3 * two), two)
    middle = pl.multiple_of(jnp.where(even, 3 * two, two), two)
    places = [pl.ds(at, two) for at in (0, edge, 2 * two, middle, 4 * two)]

    def attend(blocks, step):
        whole = blocks == 2 * CHUNKS - 1
        k_aug[:, width:] = k_seg[...]
        for at, kv in zip(places, (kv4, kv_edge, kv2, kv_middle, kv0)):
            k_aug[at, :width] = kv[:, :width]
            v_win[at] = kv[:, width:]
            k_t[:, at] = kv[:, :width].T
            v_t[:width, at] = kv[:, width:].T

        v_t[width:] = jnp.ones((v_t.shape[0] - width, v_t.shape[1]), BF)

        lane = lax.broadcasted_iota(jnp.int32, (rows, two), 1)
        causal = lax.broadcasted_iota(jnp.int32, (rows, two), 0) <= jnp.where(lane >= rows, lane - rows, lane)

        def window(u):
            first = (u // pairs + 2 * CHUNKS - 1 - blocks) * rows
            return first, slice(first, first + blocks * rows)

        def columns(u):
            return slice(u * two, (u + 1) * two)

        def fold(x, op):
            return op(x.reshape(x.shape[0] // 8, 8, x.shape[1]), axis=0)

        def scores(u, b, top):
            first, _ = window(u)
            s = dot(k_aug[first + b * rows:first + (b + step) * rows], q_t[base + u])
            for i in range(step):
                part = s[i * rows:(i + 1) * rows]
                if b + i == blocks - 1:
                    part = jnp.where(causal, part, MASKED)
                s_scr[u % 2, (b + i) * rows:(b + i + 1) * rows] = part
                top = jnp.maximum(top, fold(part, jnp.max))
            return top

        def weights(u, b, peak):
            first, _ = window(u)
            e = jnp.exp2((s_scr[u % 2, b * rows:(b + 1) * rows] - peak) * (scale * math.log2(math.e)))
            p_scr[first + b * rows:first + (b + 1) * rows, columns(u)] = e.astype(BF)

        def score_grads(u, b, inner):
            first, _ = window(u)
            keys = slice(first + b * rows, first + (b + step) * rows)
            dp = dot(v_win[keys], g_t[base + u])
            d_scr[keys, columns(u)] = p_scr[keys, columns(u)] * (dp - inner).astype(BF)

        def store(x, out, u):
            block, p = u // pairs, u % pairs
            x = x.T
            for i in range(2):
                out[block * rows:(block + 1) * rows, (2 * p + i) * width:(2 * p + i + 1) * width] = (
                    x[i * rows:(i + 1) * rows]
                )

        def query_grad(u, inv):
            _, keys = window(u)
            store((dot(k_t[:, keys], d_scr[keys, columns(u)]) * (inv * scale)).astype(BF), dq_scr, u)

        first_group = [(b * rows, *one[:3]) for b in range(blocks) for one in sums] if whole else []
        second_group = [(rows + b * rows, *one[:3]) for b in range(blocks) for one in sums] if whole else []

        def key_grads(turn):
            if turn > pairs and first_group:
                at, left, right, acc = first_group.pop(0)
                at = slice(at, at + rows)
                acc[at] = dot(left[at, :half], right[:half])
            elif turn > 3 * pairs // 2 and second_group:
                at, left, right, acc = second_group.pop(0)
                at = slice(at, at + rows)
                acc[at] += dot(left[at, half:part], right[half:part])

        def outputs(u):
            _, keys = window(u)
            o = dot(v_t[:, keys], p_scr[keys, columns(u)])
            inv = 1.0 / o[width:width + 1]
            o = (o[:width] * inv).astype(BF)
            store(o, o_scr, u)
            inner = jnp.sum(g_t[base + u].astype(F32) * o.astype(F32), axis=0, keepdims=True)
            column = jnp.broadcast_to(inv, (8, two)).T[:, :1]
            here, there = slice(u * two, (u + 1) * two), slice((base + u) * two, (base + u + 1) * two)
            qs_st[here] = (q_st[there].astype(F32) * column).astype(BF)
            gs_st[here] = (g_st[there].astype(F32) * column).astype(BF)
            return inv, inner

        def turn(u, peak, inv, inner):
            top = jnp.full((8, two), MASKED, F32)
            for b in range(0, blocks, step):
                if u + 1 < units:
                    top = scores(u + 1, b, top)
                if 0 <= u < units:
                    for i in range(step):
                        weights(u, b + i, peak)
                if u > 0:
                    score_grads(u - 1, b, inner)
                key_grads(u)
                if u + 1 >= units:
                    key_grads(u)
            if u > 0:
                query_grad(u - 1, inv)
            if 0 <= u < units:
                inv, inner = outputs(u)
            return jnp.max(top, axis=0, keepdims=True), inv, inner

        if whole:
            for one in sums:
                one[2][blocks * rows:] = jnp.zeros((rows, width), F32)
        state = (None, None, None)
        for u in range(-1, units + 1):
            state = turn(u, *state)

        mine = pl.ds(pl.multiple_of(core * rows, rows), rows)
        other = pl.ds(pl.multiple_of((1 - core) * rows, rows), rows)
        cols = pl.ds(pl.multiple_of((core * heads + slot) * wide, wide), wide)
        moves = [
            (o_scr.at[other], sent.at[:, pl.ds(0, wide)]),
            (dq_scr.at[other], sent.at[:, pl.ds(wide, wide)]),
            (o_scr.at[mine], o_all.at[:, cols]),
            (dq_scr.at[mine], dq_all.at[:, cols]),
        ]
        copies = run(moves, sems)

        for left, right, acc, factor, col in sums:
            cols = slice(col, col + width)
            late = 3 * two
            if not whole:
                acc[:late] = jnp.zeros((late, width), F32)
                acc[late:] = dot(left[late:, half:], right[half:])
                acc[late:late + 3 * rows] += dot(left[late:late + 3 * rows, :half], right[:half])

            def total(keys):
                return factor * (acc[keys] + dot(left[keys, part:], right[part:]) if whole else acc[keys])

            d4[:rows, cols] = (factor * acc[:rows]).astype(d4.dtype)
            d4[rows:, cols] = total(slice(rows, two)).astype(d4.dtype)
            for at, out in zip(places[1:], (d_edge, d2, d_middle, d0)):
                out[:, cols] = total(at).astype(out.dtype)
        for copy in copies:
            copy.wait()

    @pl.when(chip >= 2)
    def _():
        attend(2 * CHUNKS - 1, 1)

    @pl.when(chip < 2)
    def _():
        attend(4, 1)


def place_kernel(heads, o_in, dq_in, *refs):
    backs = refs[:heads]
    mine, theirs, o, dq, dk, dv, sems = refs[heads:]
    core, _ = position()
    wide = backs[0].shape[1] // 2
    half = mine.shape[1] // 2
    moves = []
    for s, back in enumerate(backs):
        cols = pl.ds(pl.multiple_of(((1 - core) * heads + s) * wide, wide), wide)
        moves += [(back.at[:, pl.ds(0, wide)], o.at[:, cols]), (back.at[:, pl.ds(wide, wide)], dq.at[:, cols])]
    for part, owner in ((mine, core), (theirs, 1 - core)):
        cols = pl.ds(pl.multiple_of(owner * half, half), half)
        moves += [(part.at[:, pl.ds(0, half)], dk.at[:, cols]), (part.at[:, pl.ds(half, half)], dv.at[:, cols])]
    for copy in run(moves, sems):
        copy.wait()


def shares(k, v, q, g):
    return pl.pallas_call(
        share_kernel,
        in_specs=[ANYWHERE] * 4,
        out_specs=[VMEM] * 3,
        out_shape=[jax.ShapeDtypeStruct(x.shape, BF) for x in (k, v, q)],
        scratch_shapes=[pltpu.SemaphoreType.DMA((6,))],
        compiler_params=pltpu.CompilerParams(vmem_limit_bytes=4 * 1024 * 1024),
        name="share",
    )(in_hbm(k), in_hbm(v), in_hbm(q), in_hbm(g))


def payloads(kv_own, kv_oth, sent, heads):
    kv = jax.ShapeDtypeStruct((2 * kv_own.shape[0], 2 * HEAD_DIM), BF)
    return pl.pallas_call(
        functools.partial(payload_kernel, heads),
        in_specs=[VMEM] * 2 + [ANYWHERE],
        out_specs=[ANYWHERE] + [VMEM] * heads,
        out_shape=[jax.ShapeDtypeStruct(sent.shape, BF)] + [kv] * heads,
        input_output_aliases={2: 0},
        compiler_params=pltpu.CompilerParams(vmem_limit_bytes=4 * 1024 * 1024),
        name="payload",
    )(kv_own, kv_oth, sent)


def staged(bounds, q, g, other, heads):
    rows = q.shape[0]
    width = HEAD_DIM
    units = q.shape[1] // (2 * width)
    return pl.pallas_call(
        functools.partial(stage_kernel, heads),
        in_specs=[ANYWHERE, ANYWHERE, ANYWHERE, VMEM],
        out_specs=[VMEM] * 5,
        out_shape=[
            jax.ShapeDtypeStruct((units * 2 * rows, width), BF),
            jax.ShapeDtypeStruct((units * 2 * rows, width), BF),
            jax.ShapeDtypeStruct((units, 2 * width, 2 * rows), BF),
            jax.ShapeDtypeStruct((units, width, 2 * rows), BF),
            jax.ShapeDtypeStruct((2 * CHUNKS * rows, width), BF),
        ],
        scratch_shapes=[
            pltpu.VMEM((rows, q.shape[1] // 2), BF),
            pltpu.VMEM((rows, q.shape[1] // 2), BF),
            pltpu.SMEM(bounds.shape, jnp.int32),
            pltpu.SemaphoreType.DMA((3,)),
        ],
        compiler_params=pltpu.CompilerParams(vmem_limit_bytes=16 * 1024 * 1024),
        cost_estimate=pl.CostEstimate(flops=0, bytes_accessed=8 * q.size, transcendentals=0),
        name="stage",
    )(in_hbm(bounds), in_hbm(q), in_hbm(g), other)


def head_attention(slot, heads, q, stage, window, so_far):
    rows = q.shape[0]
    width = HEAD_DIM
    two = 2 * rows
    units = stage[2].shape[0] // heads
    wide = q.shape[1] // (2 * heads)
    span = CHUNKS * two
    short = span - rows
    chunk = window[0].shape
    return pl.pallas_call(
        functools.partial(attention_kernel, slot, heads),
        in_specs=[VMEM] * 10 + [ANYWHERE] * len(so_far),
        out_specs=[ANYWHERE] * 3 + [VMEM] * 5,
        scratch_shapes=[
            pltpu.VMEM((span, 2 * width), BF),
            pltpu.VMEM((span, width), BF),
            pltpu.VMEM((width, span), BF),
            pltpu.VMEM((width + 16, span), BF),
            pltpu.VMEM((units * two, width), BF),
            pltpu.VMEM((units * two, width), BF),
            pltpu.VMEM((2, short, two), F32),
            pltpu.VMEM((span, units * two), BF),
            pltpu.VMEM((span, units * two), BF),
            pltpu.VMEM((span, width), F32),
            pltpu.VMEM((span, width), F32),
            pltpu.VMEM((two, wide), BF),
            pltpu.VMEM((two, wide), BF),
            pltpu.SemaphoreType.DMA((4,)),
        ],
        out_shape=[
            jax.ShapeDtypeStruct(q.shape, BF),
            jax.ShapeDtypeStruct(q.shape, BF),
            jax.ShapeDtypeStruct((rows, 2 * wide), BF),
        ] + [jax.ShapeDtypeStruct(chunk, t) for t in (BF, BF, F32, BF, F32)],
        input_output_aliases={10 + i: i for i in range(len(so_far))},
        compiler_params=pltpu.CompilerParams(vmem_limit_bytes=36 * 1024 * 1024),
        cost_estimate=pl.CostEstimate(
            flops=20 * rows * span * wide,
            bytes_accessed=24 * rows * wide,
            transcendentals=2 * rows * span * wide // width,
        ),
        name="attention%d" % slot,
    )(*stage, *window, *so_far)


def place(o, dq, backs, mine, theirs):
    heads = len(backs)
    return pl.pallas_call(
        functools.partial(place_kernel, heads),
        in_specs=[ANYWHERE] * (4 + heads),
        out_specs=[ANYWHERE] * 4,
        scratch_shapes=[pltpu.SemaphoreType.DMA((2 * heads + 4,))],
        out_shape=[
            jax.ShapeDtypeStruct(o.shape, BF),
            jax.ShapeDtypeStruct(dq.shape, BF),
            jax.ShapeDtypeStruct(mine.shape, BF),
            jax.ShapeDtypeStruct(mine.shape, BF),
        ],
        input_output_aliases={0: 0, 1: 1},
        compiler_params=pltpu.CompilerParams(vmem_limit_bytes=1024 * 1024),
        name="place",
    )(o, dq, *backs, mine, theirs)


def body(query_rows, key_rows, value_rows, grad_out, doc_bounds):
    core, chip = position()
    n = lax.axis_size("context")
    even = lax.rem(chip, 2) == 0
    rows = query_rows.shape[0]
    width = HEAD_DIM
    heads = key_rows.shape[1] // (2 * width)

    def shift(x, by):
        return lax.ppermute(x, "context", [(i, (i + by) % n) for i in range(n)])

    def swap(x):
        return lax.ppermute(x, "context", [(i, i ^ 1) for i in range(n)])

    def across(x):
        return lax.ppermute(x, "context", [(i, i ^ 2) for i in range(n)])

    kv_own, kv_sent, sent = shares(key_rows, value_rows, query_rows, grad_out)
    sent, *kv = payloads(kv_own, swap(kv_sent), sent, heads)
    stage = staged(doc_bounds, query_rows, grad_out, swap(sent), heads)

    o, dq, outs = None, None, []
    for s in range(heads):
        back2 = shift(kv[s], 4)
        edge = shift(jnp.where(even, kv[s], back2), 2)
        middle = across(back2)
        back4 = shift(back2, 4)
        o, dq, *rest = head_attention(
            s, heads, query_rows, stage, (back4, edge, back2, middle, kv[s]), () if s == 0 else (o, dq)
        )
        outs.append(rest)
    grads, backs = [], []
    for sent, d4, d_edge, d2, d_middle, d0 in outs:
        from_edge = shift(d_edge, -2)
        from_four = shift(d4, -4)
        from_middle = across(d_middle)
        d2 = jnp.where(even, d2, d2 + from_edge)
        from_two = shift((d2 + from_middle + from_four).astype(BF), -4)
        total = jnp.where(even, d0 + from_edge, d0) + from_two.astype(F32)
        grads.append(total.astype(BF))
        backs.append(swap(sent))
    total = jnp.concatenate([g[:, :width] for g in grads] + [g[:, width:] for g in grads], axis=1)
    mine = lax.dynamic_slice_in_dim(total, core * rows, rows, 0)
    theirs = swap(lax.dynamic_slice_in_dim(total, (1 - core) * rows, rows, 0))
    return place(o, dq, backs, mine, theirs)


def solution(mesh):
    rows = P(("dp", "context"), None)
    return jax.shard_map(
        body,
        mesh=mesh,
        in_specs=(rows, rows, rows, rows, P("dp")),
        out_specs=(rows, rows, rows, rows),
        check_vma=False,
    )
```
